32 devices in a mesh: groups: 2 (over y), tensor: 4 (over z), dp: 4 (over x, core).
Axes of the slice: x: 2, y: 2, z: 4, core: 2. Of those that a mesh axis runs over, the one named last changes fastest.
Arguments:
- root_features: bfloat16 [32, 16384], P('groups', 'dp'), parts along dimension 0, may hold values from -6 to 6
- branch_embeds: bfloat16 [32, 4, 8, 16384], P('groups', None, None, 'dp'), parts along dimension 0, may hold values from -6 to 6
- parents: int32 [32, 3, 8], P('groups'), parts along dimension 0, may hold values from 0 to 7
- cache_lengths: int32 [32], P(('groups', 'dp')), parts along dimension 0, may hold values from 128 to 512, as said below
- cache_kv: bfloat16 [32, 2, 512, 512], P(('groups', 'dp'), None, None, 'tensor'), parts along dimension 0, may hold values from -6 to 6, as said below
- norm_gain: bfloat16 [16384], P('dp'), may hold values from 0.099609375 to 1.8984375
- w_query: bfloat16 [16384, 2048], P('dp', 'tensor'), may hold values from -1 to 1
- w_keyval: bfloat16 [16384, 2, 512], P('dp', None, 'tensor'), may hold values from -1 to 1, as said below
- w_out: bfloat16 [2048, 16384], P('tensor', 'dp'), may hold values from -0.125 to 0.125
Outputs:
- tree_features: bfloat16 [32, 4, 8, 16384], P('groups', None, None, ('dp', 'tensor')), parts along dimension 0
The draws below stay inside these ranges and needn't reach their ends.
There are 2 independent parts, one for each index of `groups`. The reference program is written for one: setup_inputs(seed, part) draws one part's arguments, and reference() takes and returns one part's arrays. A program takes and returns all parts, laid end to end along the dimension named above; an argument that names none is the same for every part. Nothing has to cross between parts.
Inputs may be any that keep to these rules, and one draw needn't show every extreme that they name: `cache_lengths`: some request has exactly 512 valid cache positions and some other exactly 128. `cache_kv`: for each request, keys and values, the 4 blocks of 128 columns k * 4 .. (k + 1) * 4 - 1 are equal; they hold key-value head k. `w_keyval`: for keys and values, the 4 blocks of 128 columns k * 4 .. (k + 1) * 4 - 1 are equal; they hold key-value head k.
All inputs are finite; a program needn't handle non-finite values.
Results may differ from the reference program's by a relative error of at most 0.017.
Values may be sent and summed in bfloat16 or wider, within the bound.
No kernel may reach another device: no remote copies, remote signals or barrier semaphores. Data moves between devices by JAX's collectives and lax.ppermute only.
A program may use at most 128 MiB of HBM per device.

```python
import jax
import jax.numpy as jnp
from jax import lax

D = 16384
HD = 128
HEADS_DEV = 4
BRANCH = 8
DEPTHS = 4
CACHE = 512
REQUESTS = 16
HEADS = 16
KV = 1
COPIES = 4
N_TENSOR = 4


def draw_cache_lengths(key, part):
    first, second, third = jax.random.split(jax.random.fold_in(key, 17), 3)
    lengths = jax.random.randint(first, (REQUESTS,), CACHE // 4, CACHE + 1, dtype=jnp.int32)
    longest = jax.random.randint(second, (), 0, REQUESTS, dtype=jnp.int32)
    offset = jax.random.randint(third, (), 1, REQUESTS, dtype=jnp.int32)
    shortest = (longest + offset) % REQUESTS
    index_row = jnp.arange(REQUESTS, dtype=jnp.int32)
    lengths = jnp.where(index_row == shortest, CACHE // 4, lengths)
    return jnp.where(index_row == longest, CACHE, lengths).astype(jnp.int32)


def draw_cache_kv(key, part):
    entries = jax.random.normal(jax.random.fold_in(key, 37), (REQUESTS, 2, CACHE, KV, 1, HD), jnp.float32)
    entries = jnp.clip(entries, -6.0, 6.0)
    copied = jnp.broadcast_to(entries, (REQUESTS, 2, CACHE, KV, COPIES, HD))
    return copied.reshape(REQUESTS, 2, CACHE, KV * COPIES * HD).astype(jnp.bfloat16)


def shared_blocks(key):
    key_seed, value_seed = jax.random.split(jax.random.fold_in(key, 29), 2)
    key_block = jnp.clip(jax.random.normal(key_seed, (D, KV, HD), jnp.float32), -6.0, 6.0)
    value_block = jnp.clip(jax.random.normal(value_seed, (D, KV, HD), jnp.float32), -6.0, 6.0)
    return (key_block, value_block)


def draw_w_keyval(key, part):
    key_block, value_block = shared_blocks(key)
    stacked = jnp.stack([key_block, value_block], axis=1) * D ** (-0.5)
    copied = jnp.broadcast_to(stacked[:, :, :, None, :], (D, 2, KV, COPIES, HD))
    return jnp.clip(copied, -1.0, 1.0).reshape(D, 2, KV * COPIES * HD).astype(jnp.bfloat16)


def draw_w_query(key, part):
    base_seed = jax.random.fold_in(jax.random.fold_in(key, 31), 0)
    total = jnp.clip(jax.random.normal(base_seed, (D, HEADS, HD), jnp.float32), -6.0, 6.0)
    return jnp.clip(total * D ** (-0.5), -1.0, 1.0).reshape(D, HEADS * HD).astype(jnp.bfloat16)


def touch_ends(values, key, smallest, top_value):
    spot = [jax.random.randint(jax.random.fold_in(key, axis), (), 0, length) for axis, length in enumerate(values.shape)]
    widest = values.shape.index(max(values.shape))
    neighbour = spot[:widest] + [(spot[widest] + 1) % values.shape[widest]] + spot[widest + 1:]
    return values.at[tuple(spot)].set(smallest).at[tuple(neighbour)].set(top_value)


def levels(key, shape, pieces, smallest, high):
    def one(position, shards_of):
        steps = jax.random.uniform(jax.random.fold_in(jax.random.fold_in(key, 6), position), (shards_of,), jnp.float32, smallest / len(pieces), high / len(pieces))
        return jnp.repeat(jnp.exp(steps), shape[position] // shards_of).reshape((-1,) + (1,) * (len(shape) - position - 1))

    level = one(*pieces[0])
    for cut in pieces[1:]:
        level = level * one(*cut)
    return level


def gaussian(own_key, extent, spread, reach, pieces=(), held_as=jnp.bfloat16):
    factor_of = levels(own_key, extent, pieces, -0.22, 0.18) if pieces else 1.0
    array = jax.random.normal(own_key, extent, jnp.float32) * spread * factor_of
    return jnp.minimum(jnp.maximum(array, -reach), reach).astype(held_as)


def setup_inputs(seed: int = 0, part: int = 0) -> dict:
    arg_keys = jax.random.split(jax.random.key(seed), 10)
    part_keys = jax.random.split(jax.random.fold_in(arg_keys[9], part), 10)
    return {
        "root_features": gaussian(part_keys[0], (REQUESTS, D), 1.0, 6.0, ((1, 4),)),
        "branch_embeds": gaussian(part_keys[1], (REQUESTS, DEPTHS, BRANCH, D), 1.0, 6.0, ((3, 4),)),
        "parents": touch_ends(jax.random.randint(part_keys[2], (REQUESTS, DEPTHS - 1, BRANCH), 0, BRANCH), jax.random.fold_in(part_keys[2], 1), 0, BRANCH - 1).astype(jnp.int32),
        "cache_lengths": draw_cache_lengths(jax.random.fold_in(jax.random.fold_in(arg_keys[9], part), 71), part),
        "cache_kv": draw_cache_kv(jax.random.fold_in(jax.random.fold_in(arg_keys[9], part), 71), part),
        "norm_gain": jnp.clip(1.0 + 0.18 * jax.random.normal(arg_keys[5], (D,), jnp.float32), 0.099609375, 1.8984375).astype(jnp.bfloat16),
        "w_query": draw_w_query(jax.random.fold_in(arg_keys[9], 71), part),
        "w_keyval": draw_w_keyval(jax.random.fold_in(arg_keys[9], 71), part),
        "w_out": gaussian(arg_keys[8], (HEADS * HD, D), (HEADS * HD) ** -0.5, 0.125, ((0, 4), (1, 4))),
    }


epsilon = 1e-05
masked_score = -1e+30

def ancestor_path(parent_table, tree_level):
    current = jnp.broadcast_to(jnp.arange(BRANCH, dtype=jnp.int32)[None, :], (parent_table.shape[0], BRANCH))
    path_nodes = [current]
    for upper in range(tree_level, 0, -1):
        current = jnp.take_along_axis(parent_table[:, upper - 1], current, axis=1)
        path_nodes.append(current)
    return path_nodes[::-1]

def tree_mask_of(parent_table, tree_level):
    path_nodes = ancestor_path(parent_table, tree_level)
    columns = jnp.arange(BRANCH, dtype=jnp.int32)
    blocks = []
    for other_level in range(DEPTHS):
        if other_level <= tree_level:
            blocks.append(columns[None, None, :] == path_nodes[other_level][:, :, None])
        else:
            blocks.append(jnp.zeros((parent_table.shape[0], BRANCH, BRANCH), dtype=bool))
    return jnp.concatenate(blocks, axis=2)

def attend_one(packed):
    queries, cache_keys, cache_values, tree_keys, tree_values, cache_valid, tree_mask = packed
    kv_heads = cache_keys.shape[1]
    grouped = queries.astype(jnp.float32).reshape(BRANCH, kv_heads, -1, HD)
    cache_scores = jnp.einsum('bkgd,ckd->kgbc', grouped, cache_keys.astype(jnp.float32)) * HD ** (-0.5)
    tree_scores = jnp.einsum('bkgd,tkd->kgbt', grouped, tree_keys.astype(jnp.float32)) * HD ** (-0.5)
    cache_scores = jnp.where(cache_valid[None, None, None, :], cache_scores, masked_score)
    tree_scores = jnp.where(tree_mask[None, None, :, :], tree_scores, masked_score)
    row_max = jnp.maximum(lax.optimization_barrier(jnp.max(cache_scores, axis=3)), lax.optimization_barrier(jnp.max(tree_scores, axis=3)))[..., None]
    cache_exp = jnp.exp(cache_scores - row_max)
    tree_exp = jnp.exp(tree_scores - row_max)
    denominator = lax.optimization_barrier(jnp.sum(cache_exp, axis=3, keepdims=True)) + lax.optimization_barrier(jnp.sum(tree_exp, axis=3, keepdims=True))
    cache_weights = (cache_exp / denominator).astype(jnp.bfloat16)
    tree_weights = (tree_exp / denominator).astype(jnp.bfloat16)
    mixed = jnp.einsum('kgbc,ckd->bkgd', cache_weights.astype(jnp.float32), cache_values.astype(jnp.float32))
    mixed = mixed + jnp.einsum('kgbt,tkd->bkgd', tree_weights.astype(jnp.float32), tree_values.astype(jnp.float32))
    return mixed.reshape(BRANCH, -1).astype(jnp.bfloat16)

def reference(root_features, branch_embeds, parents, cache_lengths, cache_kv, norm_gain, w_query, w_keyval, w_out):
    request_count = root_features.shape[0]
    kv_heads = KV
    kv_cols = kv_heads * HD
    all_rows = request_count * BRANCH
    first_copy = cache_kv.reshape(request_count, 2, CACHE, kv_heads, COPIES, HD)[:, :, :, :, 0]
    cache_keys = first_copy[:, 0]
    cache_values = first_copy[:, 1]
    positions = jnp.arange(CACHE, dtype=jnp.int32)
    cache_valid = positions[None, :] < cache_lengths[:, None]
    tree_keys = jnp.zeros((request_count, DEPTHS * BRANCH, kv_heads, HD), jnp.bfloat16)
    tree_values = jnp.zeros((request_count, DEPTHS * BRANCH, kv_heads, HD), jnp.bfloat16)
    keyval_weight = w_keyval.reshape(D, 2, kv_heads, COPIES, HD)[:, :, :, 0].reshape(D, 2 * kv_cols)
    out_blocks = w_out.reshape(N_TENSOR, HEADS_DEV * HD, D)
    gain = norm_gain.astype(jnp.float32)
    results = []
    previous = None
    for tree_level in range(DEPTHS):
        if tree_level == 0:
            parent = jnp.broadcast_to(root_features[:, None, :], (request_count, BRANCH, D))
        else:
            parent = jnp.take_along_axis(previous, parents[:, tree_level - 1][:, :, None], axis=1)
        node_state = parent.astype(jnp.float32) + branch_embeds[:, tree_level].astype(jnp.float32)
        flat_state = node_state.reshape(all_rows, D)
        inv_rms = lax.rsqrt(lax.optimization_barrier(jnp.mean(flat_state * flat_state, axis=1, keepdims=True)) + epsilon)
        scaled = (flat_state * gain).astype(jnp.bfloat16)
        queries = (jnp.dot(scaled, w_query, preferred_element_type=jnp.float32) * inv_rms).astype(jnp.bfloat16)
        keyval = (jnp.dot(scaled, keyval_weight, preferred_element_type=jnp.float32) * inv_rms).astype(jnp.bfloat16)
        new_keys = keyval[:, :kv_cols].reshape(request_count, BRANCH, kv_heads, HD)
        new_values = keyval[:, kv_cols:].reshape(request_count, BRANCH, kv_heads, HD)
        tree_keys = tree_keys.at[:, tree_level * BRANCH:(tree_level + 1) * BRANCH].set(new_keys)
        tree_values = tree_values.at[:, tree_level * BRANCH:(tree_level + 1) * BRANCH].set(new_values)
        tree_mask = tree_mask_of(parents, tree_level)
        attended = lax.map(attend_one, (queries.reshape(request_count, BRANCH, -1), cache_keys, cache_values, tree_keys, tree_values, cache_valid, tree_mask))
        head_groups = jnp.swapaxes(attended.reshape(all_rows, N_TENSOR, HEADS_DEV * HD), 0, 1)

        def add_group(carry, pair):
            group_rows, group_weight = pair
            partial_sum = jnp.dot(group_rows, group_weight, preferred_element_type=jnp.float32).astype(jnp.bfloat16)
            partial_sum = lax.optimization_barrier(partial_sum)
            return (carry + partial_sum.astype(jnp.float32), None)
        summed, _ = lax.scan(add_group, jnp.zeros((all_rows, D), jnp.float32), (head_groups, out_blocks))
        fresh = (flat_state + summed).astype(jnp.bfloat16).reshape(request_count, BRANCH, D)
        results.append(fresh)
        previous = fresh
    return jnp.stack(results, axis=1)
```

```python
import functools

import jax
import jax.numpy as jnp
from jax import lax
from jax.experimental import pallas as pl
from jax.experimental.pallas import tpu as pltpu
from jax.sharding import PartitionSpec as P

HD = 128
BATCHES = 2
EPSILON = 1e-05
MASKED = -1e30
LANES = 128
VMEM_BYTES = 40 * 1024 * 1024


def swap(x, axis, step):
    size = lax.axis_size(axis)
    return lax.ppermute(x, axis, [(i, i ^ step) for i in range(size)])


def parent_rows(index_ref, features):
    rows, width = index_ref.shape[0], features.shape[0]
    column = lax.broadcasted_iota(jnp.int32, (rows, width), 1)
    chosen = jnp.where(column == index_ref[...], 1.0, 0.0).astype(jnp.bfloat16)
    return jnp.dot(chosen, features, preferred_element_type=jnp.float32)


def embed_rows(places_ref, embed_ref):
    dp, _, per_block = embed_ref.shape[:3]
    blocks = []
    for step in range(dp):
        for request in range(per_block):
            block = embed_ref[places_ref[step], 0, request, 0]
            blocks.append(block.astype(jnp.float32))
    return jnp.concatenate(blocks, axis=0)


def project_kernel(pieces, dp, share_ref, places_ref, index_ref, *refs):
    features = refs[:pieces]
    embed_ref, gain_ref, query_ref, keyval_ref = refs[pieces : pieces + 4]
    out_refs = refs[pieces + 4 : pieces + 4 + dp]
    held_ref, total_ref, square_ref = refs[pieces + 4 + dp :]
    step = pl.program_id(0)
    head_cols = query_ref.shape[1]

    if pieces == 1:
        held_ref[...] = features[0][...]
    else:
        for piece in range(pieces):

            @pl.when(step == piece)
            def _():
                held_ref[...] = features[piece][...]

    state = parent_rows(index_ref, held_ref[...]) + embed_rows(places_ref, embed_ref)
    squares = jnp.sum(state * state, axis=1, keepdims=True)
    scaled = (state * gain_ref[...].astype(jnp.float32)).astype(jnp.bfloat16)
    query = jnp.dot(scaled, query_ref[...], preferred_element_type=jnp.float32)
    keyval = jnp.dot(scaled, keyval_ref[...], preferred_element_type=jnp.float32)

    @pl.when(step == 0)
    def _():
        total_ref[:, :head_cols] = query
        total_ref[:, head_cols:] = keyval
        square_ref[...] = squares

    @pl.when(step > 0)
    def _():
        total_ref[:, :head_cols] += query
        total_ref[:, head_cols:] += keyval
        square_ref[...] += squares

    @pl.when(step == pl.num_programs(0) - 1)
    def _():
        width = total_ref.shape[1]
        rows = out_refs[0].shape[0]
        lane = lax.broadcasted_iota(jnp.int32, (rows, LANES), 1)
        for block in range(dp):
            span = slice(block * rows, (block + 1) * rows)
            high = square_ref[span, :].astype(jnp.bfloat16).astype(jnp.float32)
            low = square_ref[span, :] - high
            tail = jnp.where(lane == 0, high, jnp.where(lane == 1, low, 0.0))
            out_refs[block][:, :width] = total_ref[span, :].astype(jnp.bfloat16)
            out_refs[block][:, width:] = tail.astype(jnp.bfloat16)


def attend_kernel(
    dp, earlier, head_cols, model_width, base, length_ref, *refs
):
    parts = refs[:dp]
    mask_ref, cache_ref = refs[dp : dp + 2]
    earlier_refs = refs[dp + 2 : dp + 2 + earlier]
    out_ref, fresh_ref = refs[dp + 2 + earlier :]
    total = parts[0][...].astype(jnp.float32)
    for part in parts[1:]:
        total = total + part[...].astype(jnp.float32)
    width = head_cols + fresh_ref.shape[1]
    squares = jnp.sum(total[:, width:], axis=1, keepdims=True)
    inv_rms = lax.rsqrt(squares / model_width + EPSILON)
    projected = (total[:, :width] * inv_rms).astype(jnp.bfloat16).astype(jnp.float32)
    fresh = projected[:, head_cols:]
    fresh_ref[...] = fresh
    per_block, _, cache, kv_cols = cache_ref.shape[1:]
    branch = total.shape[0] // per_block
    kv_heads = kv_cols // HD
    group = head_cols // HD // kv_heads
    positions = mask_ref.shape[1]
    tree = [ref[...] for ref in earlier_refs] + [fresh]
    blank = jnp.zeros((positions - branch * len(tree), HD), jnp.float32)
    column = lax.broadcasted_iota(jnp.int32, (group * branch, cache), 1)
    across = (((1,), (1,)), ((), ()))
    outs = []
    for request in range(per_block):
        span = slice(request * branch, (request + 1) * branch)
        valid = column < length_ref[base + request]
        allowed = jnp.concatenate([mask_ref[span, :]] * group, axis=0) > 0.5
        heads = []
        for kv in range(kv_heads):
            first = kv * group
            queries = jnp.concatenate(
                [
                    projected[span, (first + g) * HD : (first + g + 1) * HD]
                    for g in range(group)
                ],
                axis=0,
            ).astype(jnp.bfloat16)
            key_cols = slice(kv * HD, (kv + 1) * HD)
            value_cols = slice(kv_cols + kv * HD, kv_cols + (kv + 1) * HD)
            filler = [blank] if blank.shape[0] else []
            tree_keys = jnp.concatenate(
                [level[span, key_cols] for level in tree] + filler, axis=0
            ).astype(jnp.bfloat16)
            tree_values = jnp.concatenate(
                [level[span, value_cols] for level in tree] + filler, axis=0
            ).astype(jnp.bfloat16)
            keys = cache_ref[0, request, 0, :, key_cols]
            values = cache_ref[0, request, 1, :, key_cols]
            scale = HD**-0.5
            near = lax.dot_general(
                queries, keys, across, preferred_element_type=jnp.float32
            )
            far = lax.dot_general(
                queries, tree_keys, across, preferred_element_type=jnp.float32
            )
            near = jnp.where(valid, near * scale, MASKED)
            far = jnp.where(allowed, far * scale, MASKED)
            top = jnp.maximum(
                jnp.max(near, axis=1, keepdims=True), jnp.max(far, axis=1, keepdims=True)
            )
            near = jnp.exp(near - top)
            far = jnp.exp(far - top)
            below = jnp.sum(near, axis=1, keepdims=True) + jnp.sum(far, axis=1, keepdims=True)
            mixed = jnp.dot(
                (near / below).astype(jnp.bfloat16), values, preferred_element_type=jnp.float32
            ) + jnp.dot(
                (far / below).astype(jnp.bfloat16), tree_values, preferred_element_type=jnp.float32
            )
            heads += [mixed[g * branch : (g + 1) * branch] for g in range(group)]
        outs.append(jnp.concatenate(heads, axis=1))
    out_ref[...] = jnp.concatenate(outs, axis=0).astype(jnp.bfloat16)


def output_kernel(dp, weights, has_alias, info_ref, index_ref, *refs):
    attended = refs[:dp]
    weight_refs = refs[dp : dp + len(weights)]
    feature_ref, embed_ref = refs[dp + len(weights) : dp + len(weights) + 2]
    rest = refs[dp + len(weights) + 2 + has_alias :]
    fresh_ref, out_ref, gathered_ref = rest
    rows = attended[0].shape[0]
    for step in range(dp):
        gathered_ref[step * rows : (step + 1) * rows, :] = attended[step][...]
    fresh = parent_rows(index_ref, feature_ref[...]) + embed_rows(info_ref, embed_ref)
    for weight_ref, (start, side) in zip(weight_refs, weights):
        depth = weight_ref.shape[0]
        if side is None:
            left = gathered_ref[:, start : start + depth]
        else:
            offset = pl.multiple_of(start + info_ref[dp + side], LANES)
            left = gathered_ref[:, pl.ds(offset, depth)]
        fresh = fresh + jnp.dot(left, weight_ref[...], preferred_element_type=jnp.float32)
    fresh_ref[...] = fresh.astype(jnp.bfloat16)
    per_block, branch = out_ref.shape[2], out_ref.shape[4]
    for step in range(dp):
        for request in range(per_block):
            start = (step * per_block + request) * branch
            out_ref[info_ref[step], 0, request, 0] = fresh[start : start + branch].astype(
                jnp.bfloat16
            )


def project(level, batch, share_ids, places, index, pieces, embeds, gain, w_query, w_keyval):
    dp, _, per_block, _, branch, feat_cols = embeds.shape
    steps = share_ids.shape[0]
    cols = feat_cols // steps
    head_cols, kv_cols = w_query.shape[1], w_keyval.shape[1]
    rows = per_block * branch
    if len(pieces) == 1:
        piece_specs = [
            pl.BlockSpec((pieces[0].shape[0], cols), lambda k, s, p: (0, s[k])),
        ]
    else:
        piece_specs = [pl.BlockSpec(x.shape, lambda k, s, p: (0, 0)) for x in pieces]
    width = head_cols + kv_cols + LANES
    out_shape = [jax.ShapeDtypeStruct((rows, width), jnp.bfloat16)] * dp
    body = functools.partial(project_kernel, len(pieces), dp)
    return pl.pallas_call(
        body,
        grid_spec=pltpu.PrefetchScalarGridSpec(
            num_scalar_prefetch=2,
            grid=(steps,),
            in_specs=[pl.BlockSpec(index.shape, lambda k, s, p: (0, 0))]
            + piece_specs
            + [
                pl.BlockSpec(
                    (dp, 1, per_block, 1, branch, cols),
                    lambda k, s, p: (0, batch, 0, level, 0, s[k]),
                ),
                pl.BlockSpec((1, cols), lambda k, s, p: (0, s[k])),
                pl.BlockSpec((cols, head_cols), lambda k, s, p: (s[k], 0)),
                pl.BlockSpec((cols, kv_cols), lambda k, s, p: (s[k], 0)),
            ],
            out_specs=[pl.BlockSpec((rows, width), lambda k, s, p: (0, 0))] * dp,
            scratch_shapes=[
                pltpu.VMEM((pieces[0].shape[0], cols), jnp.bfloat16),
                pltpu.VMEM((dp * rows, head_cols + kv_cols), jnp.float32),
                pltpu.VMEM((dp * rows, 1), jnp.float32),
            ],
        ),
        out_shape=out_shape,
        compiler_params=pltpu.CompilerParams(vmem_limit_bytes=VMEM_BYTES),
        cost_estimate=pl.CostEstimate(
            flops=2 * dp * rows * feat_cols * (head_cols + kv_cols),
            bytes_accessed=2 * feat_cols * (head_cols + kv_cols + 2 * dp * rows),
            transcendentals=0,
        ),
        name="project",
    )(share_ids, places, index, *pieces, embeds, gain, w_query, w_keyval)


def attend(batch, model_width, head_cols, lengths, parts, mask, cache, earlier):
    rows, width = parts[0].shape
    fresh_cols = width - LANES - head_cols
    per_block = cache.shape[1]
    whole = lambda x: pl.BlockSpec(x.shape, lambda i, n: (0,) * x.ndim)
    cache_shape = (1,) + cache.shape[1:]
    return pl.pallas_call(
        functools.partial(
            attend_kernel,
            len(parts),
            len(earlier),
            head_cols,
            model_width,
            batch * per_block,
        ),
        grid_spec=pltpu.PrefetchScalarGridSpec(
            num_scalar_prefetch=1,
            grid=(1,),
            in_specs=[whole(x) for x in parts]
            + [whole(mask), pl.BlockSpec(cache_shape, lambda i, n: (batch, 0, 0, 0, 0))]
            + [whole(x) for x in earlier],
            out_specs=[
                pl.BlockSpec((rows, head_cols), lambda i, n: (0, 0)),
                pl.BlockSpec((rows, fresh_cols), lambda i, n: (0, 0)),
            ],
        ),
        out_shape=[
            jax.ShapeDtypeStruct((rows, head_cols), jnp.bfloat16),
            jax.ShapeDtypeStruct((rows, fresh_cols), jnp.float32),
        ],
        compiler_params=pltpu.CompilerParams(vmem_limit_bytes=VMEM_BYTES),
        cost_estimate=pl.CostEstimate(
            flops=4 * rows * head_cols * cache.shape[3],
            bytes_accessed=4 * cache.shape[3] * per_block * HD * 8,
            transcendentals=rows * head_cols * 4,
        ),
        name="attend",
    )(lengths, *parts, mask, cache, *earlier)


def output(level, batch, info, index, attended, weights, features, embeds, held, share_cols):
    dp, batches, per_block, depths, branch, _ = embeds.shape
    rows = dp * per_block * branch
    block = min(2 * LANES, share_cols)
    steps = share_cols // block
    full = lambda x: pl.BlockSpec(x.shape, lambda j, s: (0, 0))
    local = features.shape[1] == share_cols
    base = dp + 2
    if local:
        feature_map = lambda j, s: (0, j)
    else:
        feature_map = lambda j, s: (0, s[base] * steps + j)
    arrays = [w for w, _, _ in weights]
    places = [(start, side) for _, start, side in weights]
    out_shape = jax.ShapeDtypeStruct(
        (dp, batches, per_block, depths, branch, share_cols), jnp.bfloat16
    )
    in_specs = (
        [full(index)]
        + [full(x) for x in attended]
        + [pl.BlockSpec((w.shape[0], block), lambda j, s: (0, j)) for w in arrays]
        + [
            pl.BlockSpec((features.shape[0], block), feature_map),
            pl.BlockSpec(
                (dp, 1, per_block, 1, branch, block),
                lambda j, s: (0, batch, 0, level, 0, s[base] * steps + j),
            ),
        ]
    )
    operands = [info, index, *attended, *arrays, features, embeds]
    aliases = {}
    if held is not None:
        in_specs.append(pl.BlockSpec(memory_space=pl.ANY))
        aliases = {len(operands): 1}
        operands.append(held)
    depth = sum(w.shape[0] for w in arrays)
    return pl.pallas_call(
        functools.partial(output_kernel, dp, places, int(held is not None)),
        grid_spec=pltpu.PrefetchScalarGridSpec(
            num_scalar_prefetch=1,
            grid=(steps,),
            in_specs=in_specs,
            out_specs=[
                pl.BlockSpec((rows, block), lambda j, s: (0, j)),
                pl.BlockSpec(
                    (dp, 1, per_block, 1, branch, block),
                    lambda j, s: (0, batch, 0, level, 0, j),
                ),
            ],
            scratch_shapes=[pltpu.VMEM((rows, depth), jnp.bfloat16)],
        ),
        out_shape=[jax.ShapeDtypeStruct((rows, share_cols), jnp.bfloat16), out_shape],
        input_output_aliases=aliases,
        compiler_params=pltpu.CompilerParams(vmem_limit_bytes=VMEM_BYTES),
        cost_estimate=pl.CostEstimate(
            flops=2 * rows * depth * share_cols,
            bytes_accessed=2 * depth * share_cols,
            transcendentals=0,
        ),
        name="output",
    )(*operands)


def tree_masks(own_parents, depths, branch):
    columns = jnp.arange(branch, dtype=jnp.int32)
    masks = []
    for level in range(depths):
        current = jnp.broadcast_to(columns, own_parents.shape[:2] + (branch,))
        blocks = [columns == current[..., None]]
        for upper in range(level, 0, -1):
            above = own_parents[:, :, upper - 1]
            current = jnp.sum(
                jnp.where(current[..., None] == columns, above[:, :, None, :], 0), axis=3
            )
            blocks.append(columns == current[..., None])
        blocks = blocks[::-1]
        blank = jnp.zeros(blocks[0].shape, bool)
        blocks += [blank] * (depths - len(blocks))
        joined = jnp.concatenate(blocks, axis=3).astype(jnp.float32)
        masks.append(joined.reshape(own_parents.shape[0], -1, depths * branch))
    return masks


def shards(
    root_features,
    branch_embeds,
    parents,
    cache_lengths,
    cache_kv,
    norm_gain,
    w_query,
    w_keyval,
    w_out,
):
    requests, depths, branch, feat_cols = branch_embeds.shape
    dp, tensor, groups = (lax.axis_size(name) for name in ("dp", "tensor", "groups"))
    dp_index, tensor_index, group_index = (
        lax.axis_index(name).astype(jnp.int32) for name in ("dp", "tensor", "groups")
    )
    local = requests // dp
    batches = BATCHES
    per_block = local // batches
    share_cols = feat_cols // tensor
    head_cols = w_query.shape[1]
    head_rows = w_out.shape[0]
    by_swaps = tensor == 4 and groups == 2

    if by_swaps:
        half = head_rows // 2
        own = lax.dynamic_slice(w_out, (0, tensor_index * share_cols), (head_rows, share_cols))
        weights = [(own, 0, None)]
        for step in (3, 2, 1):
            sent = lax.dynamic_slice(
                w_out,
                (group_index * half, (tensor_index ^ step) * share_cols),
                (half, share_cols),
            )
            arrived = swap(sent, "tensor", step)
            weights.append((arrived, step * head_rows, 0))
            weights.append((swap(arrived, "groups", 1), step * head_rows, 1))
    else:
        half = 0
        spread = lax.all_to_all(w_out, "tensor", 1, 0, tiled=True)
        weights = [(spread, 0, None)]

    embeds = branch_embeds.reshape(dp, batches, per_block, depths, branch, feat_cols)
    gain = norm_gain.reshape(1, feat_cols)
    keyval = w_keyval.reshape(feat_cols, -1)
    cache = cache_kv.reshape((batches, per_block) + cache_kv.shape[1:])
    places = jnp.stack([dp_index ^ step for step in range(dp)])
    info = jnp.concatenate(
        [
            places,
            jnp.stack([group_index * half, (1 - group_index) * half, tensor_index]),
        ]
    )
    if by_swaps:
        share_ids = jnp.stack([tensor_index ^ step for step in range(tensor)])
    else:
        share_ids = jnp.zeros((1,), jnp.int32)
    root_ids = jnp.arange(4 if by_swaps else 1, dtype=jnp.int32)

    split = parents.reshape(dp, batches, per_block, depths - 1, branch)
    ordered = jnp.stack(
        [lax.dynamic_index_in_dim(split, dp_index ^ step, 0, False) for step in range(dp)]
    )
    slot = (
        jnp.arange(dp, dtype=jnp.int32)[:, None] * per_block
        + jnp.arange(per_block, dtype=jnp.int32)[None, :]
    )
    rows = dp * per_block * branch
    indices = []
    for level in range(depths):
        row = []
        for batch in range(batches):
            if level == 0:
                request = (
                    places[:, None] * local
                    + batch * per_block
                    + jnp.arange(per_block, dtype=jnp.int32)[None, :]
                )
                place = jnp.broadcast_to(request[:, :, None], (dp, per_block, branch))
            else:
                place = slot[:, :, None] * branch + ordered[:, batch, :, level - 1]
            row.append(place.reshape(rows, 1))
        indices.append(row)
    masks = tree_masks(ordered[0], depths, branch)

    earlier = [[] for _ in range(batches)]
    shares = [root_features] * batches
    gathered = [[root_features]] * batches
    held = None
    for level in range(depths):
        attended = []
        for batch in range(batches):
            sums = project(
                level,
                batch,
                root_ids if level == 0 else share_ids,
                places,
                indices[level][batch],
                gathered[batch],
                embeds,
                gain,
                w_query,
                keyval,
            )
            parts = [sums[0]] + [swap(sums[step], "dp", step) for step in range(1, dp)]
            mixed, fresh = attend(
                batch,
                feat_cols * dp,
                head_cols,
                cache_lengths,
                parts,
                masks[level][batch],
                cache,
                earlier[batch],
            )
            earlier[batch] = earlier[batch] + [fresh]
            if by_swaps:
                heads = [mixed] + [swap(mixed, "tensor", step) for step in range(1, tensor)]
                joined = jnp.concatenate(heads, axis=1)
            else:
                joined = lax.all_gather(mixed, "tensor", axis=1, tiled=True)
            attended.append([joined] + [swap(joined, "dp", step) for step in range(1, dp)])
        for batch in range(batches):
            shares[batch], held = output(
                level,
                batch,
                info,
                indices[level][batch],
                attended[batch],
                weights,
                shares[batch],
                embeds,
                held,
                share_cols,
            )
            if level + 1 == depths:
                continue
            own = shares[batch]
            if by_swaps:
                far = swap(own, "tensor", 3)
                gathered[batch] = [own, swap(own, "tensor", 1), swap(far, "tensor", 1), far]
            else:
                gathered[batch] = [lax.all_gather(own, "tensor", axis=1, tiled=True)]
    return held.reshape(requests, depths, branch, share_cols)


def solution(mesh):
    return jax.shard_map(
        shards,
        mesh=mesh,
        in_specs=(
            P("groups", "dp"),
            P("groups", None, None, "dp"),
            P("groups", None, None),
            P(("groups", "dp")),
            P(("groups", "dp"), None, None, "tensor"),
            P("dp"),
            P("dp", "tensor"),
            P("dp", None, "tensor"),
            P("tensor", "dp"),
        ),
        out_specs=P("groups", None, None, ("dp", "tensor")),
        check_vma=False,
    )
```

```python
import functools

import jax
import jax.numpy as jnp
from jax import lax
from jax.experimental import pallas as pl
from jax.experimental.pallas import tpu as pltpu
from jax.sharding import PartitionSpec as P

HD = 128
BATCHES = 1
CHUNKS = 2
EPSILON = 1e-05
MASKED = -1e30
LANES = 128
VMEM_BYTES = 20 * 1024 * 1024


def swap(x, axis, step):
    size = lax.axis_size(axis)
    return lax.ppermute(x, axis, [(i, i ^ step) for i in range(size)])


def parent_rows(index_ref, features):
    rows, width = index_ref.shape[0], features.shape[0]
    column = lax.broadcasted_iota(jnp.int32, (rows, width), 1)
    chosen = jnp.where(column == index_ref[...], 1.0, 0.0).astype(jnp.bfloat16)
    return jnp.dot(chosen, features, preferred_element_type=jnp.float32)


def embed_rows(places_ref, embed_ref, batch, level, columns):
    dp, _, per_block = embed_ref.shape[:3]
    blocks = []
    for step in range(dp):
        for request in range(per_block):
            block = embed_ref[places_ref[step], batch, request, level, :, columns]
            blocks.append(block.astype(jnp.float32))
    return jnp.concatenate(blocks, axis=0)


def cut_kernel(half, info_ref, weight_ref, *refs):
    outs, sems = refs[:-1], refs[-1]
    share = outs[0].shape[1]
    copies = []
    for place, out_ref in enumerate(outs):
        step, start, depth = half[place]
        row = start if step == 0 else pl.multiple_of(start + info_ref[0], 16)
        column = pl.multiple_of((info_ref[1] ^ step) * share, LANES)
        copies.append(
            pltpu.make_async_copy(
                weight_ref.at[pl.ds(row, depth), pl.ds(column, share)],
                out_ref,
                sems.at[place],
            )
        )
    for copy in copies:
        copy.start()
    for copy in copies:
        copy.wait()


def cut(info, w_out, plan, share):
    shapes = [(depth, share) for _, _, depth in plan]
    return pl.pallas_call(
        functools.partial(cut_kernel, plan),
        grid_spec=pltpu.PrefetchScalarGridSpec(
            num_scalar_prefetch=1,
            grid=(1,),
            in_specs=[pl.BlockSpec(memory_space=pl.ANY)],
            out_specs=[pl.BlockSpec(memory_space=pl.ANY) for _ in shapes],
            scratch_shapes=[pltpu.SemaphoreType.DMA((len(shapes),))],
        ),
        out_shape=[jax.ShapeDtypeStruct(shape, w_out.dtype) for shape in shapes],
        compiler_params=pltpu.CompilerParams(vmem_limit_bytes=VMEM_BYTES),
        name="cut",
    )(info, w_out)


def load_kernel(*refs):
    count = len(refs) // 2
    sources, held, sems = refs[:count], refs[count : 2 * count], refs[-1]
    copies = [
        pltpu.make_async_copy(source, target, sems.at[place])
        for place, (source, target) in enumerate(zip(sources, held))
    ]
    for copy in copies:
        copy.start()
    for copy in copies:
        copy.wait()


def load(*arrays):
    return pl.pallas_call(
        load_kernel,
        in_specs=[pl.BlockSpec(memory_space=pl.ANY) for _ in arrays],
        out_specs=[pl.BlockSpec(memory_space=pltpu.VMEM) for _ in arrays],
        out_shape=[pltpu.VMEM(x.shape, x.dtype) for x in arrays],
        scratch_shapes=[pltpu.SemaphoreType.DMA((len(arrays),))],
        compiler_params=pltpu.CompilerParams(vmem_limit_bytes=VMEM_BYTES),
        name="load",
    )(*arrays)


def project_kernel(level, batch, pieces, steps, dp, share_ref, places_ref, index_ref, *refs):
    features = refs[:pieces]
    embed_ref, gain_ref, query_ref, keyval_ref = refs[pieces : pieces + 4]
    out_refs = refs[pieces + 4 : pieces + 4 + dp]
    cols = query_ref.shape[0] // steps
    query = keyval = squares = None
    for step in range(steps):
        offset = pl.multiple_of(share_ref[step] * cols, LANES)
        columns = pl.ds(offset, cols)
        held = features[step][...] if pieces == steps else features[0][:, columns]
        state = parent_rows(index_ref, held) + embed_rows(
            places_ref, embed_ref, batch, level, columns
        )
        square = jnp.sum(state * state, axis=1, keepdims=True)
        gain = gain_ref[:, columns].astype(jnp.float32)
        scaled = (state * gain).astype(jnp.bfloat16)
        first = jnp.dot(scaled, query_ref[columns, :], preferred_element_type=jnp.float32)
        second = jnp.dot(scaled, keyval_ref[columns, :], preferred_element_type=jnp.float32)
        query = first if step == 0 else query + first
        keyval = second if step == 0 else keyval + second
        squares = square if step == 0 else squares + square
    head_cols = query.shape[1]
    width = head_cols + keyval.shape[1]
    rows = out_refs[0].shape[0]
    lane = lax.broadcasted_iota(jnp.int32, (rows, LANES), 1)
    for block in range(dp):
        span = slice(block * rows, (block + 1) * rows)
        high = squares[span].astype(jnp.bfloat16).astype(jnp.float32)
        low = squares[span] - high
        tail = jnp.where(lane == 0, high, jnp.where(lane == 1, low, 0.0))
        out_refs[block][:, :head_cols] = query[span].astype(jnp.bfloat16)
        out_refs[block][:, head_cols:width] = keyval[span].astype(jnp.bfloat16)
        out_refs[block][:, width:] = tail.astype(jnp.bfloat16)


def attend_kernel(
    dp, earlier, head_cols, model_width, base, branch, length_ref, *refs
):
    parts = refs[:dp]
    mask_ref, cache_ref = refs[dp : dp + 2]
    earlier_refs = refs[dp + 2 : dp + 2 + earlier]
    out_ref, fresh_ref = refs[dp + 2 + earlier :]
    total = parts[0][...].astype(jnp.float32)
    for part in parts[1:]:
        total = total + part[...].astype(jnp.float32)
    width = head_cols + fresh_ref.shape[1]
    squares = jnp.sum(total[:, width:], axis=1, keepdims=True)
    inv_rms = lax.rsqrt(squares / model_width + EPSILON)
    projected = (total[:, :width] * inv_rms).astype(jnp.bfloat16).astype(jnp.float32)
    fresh = projected[:, head_cols:]
    fresh_ref[...] = fresh
    _, _, cache, kv_cols = cache_ref.shape
    per_block = total.shape[0] // branch
    kv_heads = kv_cols // HD
    group = head_cols // HD // kv_heads
    positions = mask_ref.shape[1]
    tree = [ref[...] for ref in earlier_refs] + [fresh]
    blank = jnp.zeros((positions - branch * len(tree), HD), jnp.float32)
    column = lax.broadcasted_iota(jnp.int32, (group * branch, cache), 1)
    across = (((1,), (1,)), ((), ()))
    outs = []
    for request in range(per_block):
        span = slice(request * branch, (request + 1) * branch)
        valid = column < length_ref[base + request]
        allowed = jnp.concatenate([mask_ref[span, :]] * group, axis=0) > 0.5
        heads = []
        for kv in range(kv_heads):
            first = kv * group
            queries = jnp.concatenate(
                [
                    projected[span, (first + g) * HD : (first + g + 1) * HD]
                    for g in range(group)
                ],
                axis=0,
            ).astype(jnp.bfloat16)
            key_cols = slice(kv * HD, (kv + 1) * HD)
            value_cols = slice(kv_cols + kv * HD, kv_cols + (kv + 1) * HD)
            filler = [blank] if blank.shape[0] else []
            tree_keys = jnp.concatenate(
                [level[span, key_cols] for level in tree] + filler, axis=0
            ).astype(jnp.bfloat16)
            tree_values = jnp.concatenate(
                [level[span, value_cols] for level in tree] + filler, axis=0
            ).astype(jnp.bfloat16)
            keys = cache_ref[base + request, 0, :, key_cols]
            values = cache_ref[base + request, 1, :, key_cols]
            scale = HD**-0.5
            near = lax.dot_general(
                queries, keys, across, preferred_element_type=jnp.float32
            )
            far = lax.dot_general(
                queries, tree_keys, across, preferred_element_type=jnp.float32
            )
            near = jnp.where(valid, near * scale, MASKED)
            far = jnp.where(allowed, far * scale, MASKED)
            top = jnp.maximum(
                jnp.max(near, axis=1, keepdims=True), jnp.max(far, axis=1, keepdims=True)
            )
            near = jnp.exp(near - top)
            far = jnp.exp(far - top)
            below = jnp.sum(near, axis=1, keepdims=True) + jnp.sum(far, axis=1, keepdims=True)
            mixed = jnp.dot(
                (near / below).astype(jnp.bfloat16), values, preferred_element_type=jnp.float32
            ) + jnp.dot(
                (far / below).astype(jnp.bfloat16), tree_values, preferred_element_type=jnp.float32
            )
            heads += [mixed[g * branch : (g + 1) * branch] for g in range(group)]
        outs.append(jnp.concatenate(heads, axis=1))
    out_ref[...] = jnp.concatenate(outs, axis=0).astype(jnp.bfloat16)


def output_kernel(level, batch, dp, weights, keep, info_ref, index_ref, *refs):
    attended = refs[:dp]
    weight_refs = refs[dp : dp + len(weights)]
    feature_ref, embed_ref = refs[dp + len(weights) : dp + len(weights) + 2]
    rest = refs[dp + len(weights) + 2 :]
    fresh_ref, gathered_ref = rest[0], rest[-1]
    rows = attended[0].shape[0]
    share = fresh_ref.shape[1]
    for step in range(dp):
        gathered_ref[step * rows : (step + 1) * rows, :] = attended[step][...]
    spans = []
    for weight_ref, (start, side) in zip(weight_refs, weights):
        depth = weight_ref.shape[0]
        if side is not None:
            start = pl.multiple_of(start + info_ref[dp + side], LANES)
        spans.append(pl.ds(start, depth))
        if keep:
            rest[1][spans[-1], :] = weight_ref[...]
    if keep:
        weight_refs, spans = [rest[1]], [slice(None)]
    offset = pl.multiple_of(info_ref[dp + 2] * share, LANES)
    block = min(2 * LANES, share)
    for start in range(0, share, block):
        if feature_ref.shape[1] == share:
            held = feature_ref[:, start : start + block]
        else:
            held = feature_ref[:, pl.ds(offset + start, block)]
        fresh = parent_rows(index_ref, held) + embed_rows(
            info_ref, embed_ref, batch, level, pl.ds(offset + start, block)
        )
        for weight_ref, span in zip(weight_refs, spans):
            fresh = fresh + jnp.dot(
                gathered_ref[:, span],
                weight_ref[:, start : start + block],
                preferred_element_type=jnp.float32,
            )
        fresh_ref[:, start : start + block] = fresh.astype(jnp.bfloat16)


def store_kernel(info_ref, fresh_ref, *refs):
    out_ref = refs[-1]
    dp, per_block, branch = out_ref.shape[0], out_ref.shape[2], out_ref.shape[4]
    fresh = fresh_ref[...].astype(jnp.float32)
    for step in range(dp):
        for request in range(per_block):
            start = (step * per_block + request) * branch
            block = fresh[start : start + branch].astype(jnp.bfloat16)
            out_ref[info_ref[step], 0, request, 0] = block


def full(x):
    return pl.BlockSpec(x.shape, lambda i, *_: (0,) * x.ndim)


def project(level, batch, share_ids, places, index, pieces, embeds, gain, w_query, keyval):
    dp, _, per_block, _, branch, feat_cols = embeds.shape
    steps = share_ids.shape[0]
    head_cols, kv_cols = w_query.shape[1], keyval.shape[1]
    rows = per_block * branch
    width = head_cols + kv_cols + LANES
    operands = [index, *pieces, embeds, gain, w_query, keyval]
    return pl.pallas_call(
        functools.partial(project_kernel, level, batch, len(pieces), steps, dp),
        grid_spec=pltpu.PrefetchScalarGridSpec(
            num_scalar_prefetch=2,
            grid=(),
            in_specs=[pl.BlockSpec(memory_space=pltpu.VMEM)] * len(operands),
            out_specs=[pl.BlockSpec(memory_space=pltpu.VMEM)] * dp,
        ),
        out_shape=[jax.ShapeDtypeStruct((rows, width), jnp.bfloat16)] * dp,
        compiler_params=pltpu.CompilerParams(vmem_limit_bytes=VMEM_BYTES),
        cost_estimate=pl.CostEstimate(
            flops=2 * dp * rows * feat_cols * (head_cols + kv_cols),
            bytes_accessed=4 * dp * rows * feat_cols,
            transcendentals=0,
        ),
        name="project",
    )(share_ids, places, *operands)


def attend(batch, per_block, model_width, head_cols, lengths, parts, mask, cache, earlier):
    rows, width = parts[0].shape
    fresh_cols = width - LANES - head_cols
    operands = [*parts, mask, cache, *earlier]
    return pl.pallas_call(
        functools.partial(
            attend_kernel,
            len(parts),
            len(earlier),
            head_cols,
            model_width,
            batch * per_block,
            rows // per_block,
        ),
        grid_spec=pltpu.PrefetchScalarGridSpec(
            num_scalar_prefetch=1,
            grid=(),
            in_specs=[pl.BlockSpec(memory_space=pltpu.VMEM)] * len(operands),
            out_specs=[pl.BlockSpec(memory_space=pltpu.VMEM)] * 2,
        ),
        out_shape=[
            jax.ShapeDtypeStruct((rows, head_cols), jnp.bfloat16),
            jax.ShapeDtypeStruct((rows, fresh_cols), jnp.float32),
        ],
        compiler_params=pltpu.CompilerParams(vmem_limit_bytes=VMEM_BYTES),
        cost_estimate=pl.CostEstimate(
            flops=4 * rows * head_cols * cache.shape[2],
            bytes_accessed=4 * cache.shape[2] * per_block * HD,
            transcendentals=rows * head_cols * 4,
        ),
        name="attend",
    )(lengths, *operands)


def output(level, batch, info, index, attended, weights, features, embeds, share_cols):
    dp, _, per_block, _, branch, _ = embeds.shape
    rows = dp * per_block * branch
    arrays = [w for w, _, _ in weights]
    places = [(start, side) for _, start, side in weights]
    depth = sum(w.shape[0] for w in arrays)
    keep = len(weights) > 1
    operands = [index, *attended, *arrays, features, embeds]
    out_shape = [jax.ShapeDtypeStruct((rows, share_cols), jnp.bfloat16)]
    if keep:
        out_shape.append(pltpu.VMEM((depth, share_cols), jnp.bfloat16))
    return pl.pallas_call(
        functools.partial(output_kernel, level, batch, dp, places, keep),
        grid_spec=pltpu.PrefetchScalarGridSpec(
            num_scalar_prefetch=1,
            grid=(),
            in_specs=[pl.BlockSpec(memory_space=pltpu.VMEM)] * len(operands),
            out_specs=[pl.BlockSpec(memory_space=pltpu.VMEM)] * len(out_shape),
            scratch_shapes=[pltpu.VMEM((rows, depth), jnp.bfloat16)],
        ),
        out_shape=out_shape,
        compiler_params=pltpu.CompilerParams(vmem_limit_bytes=VMEM_BYTES),
        cost_estimate=pl.CostEstimate(
            flops=2 * rows * depth * share_cols,
            bytes_accessed=2 * rows * depth,
            transcendentals=0,
        ),
        name="output",
    )(info, *operands)


def store(level, batch, shape, info, fresh, held):
    dp, _, per_block, _, branch, share_cols = shape
    operands = [info, fresh]
    in_specs = [full(fresh)]
    aliases = {}
    if held is not None:
        in_specs.append(pl.BlockSpec(memory_space=pl.ANY))
        aliases = {2: 0}
        operands.append(held)
    return pl.pallas_call(
        store_kernel,
        grid_spec=pltpu.PrefetchScalarGridSpec(
            num_scalar_prefetch=1,
            grid=(1,),
            in_specs=in_specs,
            out_specs=pl.BlockSpec(
                (dp, 1, per_block, 1, branch, share_cols),
                lambda i, s: (0, batch, 0, level, 0, 0),
            ),
        ),
        out_shape=jax.ShapeDtypeStruct(shape, jnp.bfloat16),
        input_output_aliases=aliases,
        compiler_params=pltpu.CompilerParams(vmem_limit_bytes=VMEM_BYTES),
        cost_estimate=pl.CostEstimate(
            flops=0, bytes_accessed=4 * fresh.size, transcendentals=0
        ),
        name="store",
    )(*operands)


def tree_masks(own_parents, depths, branch):
    columns = jnp.arange(branch, dtype=jnp.int32)
    masks = []
    for level in range(depths):
        current = jnp.broadcast_to(columns, own_parents.shape[:2] + (branch,))
        blocks = [columns == current[..., None]]
        for upper in range(level, 0, -1):
            above = own_parents[:, :, upper - 1]
            current = jnp.sum(
                jnp.where(current[..., None] == columns, above[:, :, None, :], 0), axis=3
            )
            blocks.append(columns == current[..., None])
        blocks = blocks[::-1]
        blank = jnp.zeros(blocks[0].shape, bool)
        blocks += [blank] * (depths - len(blocks))
        joined = jnp.concatenate(blocks, axis=3).astype(jnp.float32)
        masks.append(joined.reshape(own_parents.shape[0], -1, depths * branch))
    return masks


def shards(
    root_features,
    branch_embeds,
    parents,
    cache_lengths,
    cache_kv,
    norm_gain,
    w_query,
    w_keyval,
    w_out,
):
    requests, depths, branch, feat_cols = branch_embeds.shape
    dp, tensor, groups = (lax.axis_size(name) for name in ("dp", "tensor", "groups"))
    dp_index, tensor_index, group_index = (
        lax.axis_index(name).astype(jnp.int32) for name in ("dp", "tensor", "groups")
    )
    local = requests // dp
    batches = BATCHES
    per_block = local // batches
    share_cols = feat_cols // tensor
    head_cols = w_query.shape[1]
    head_rows = w_out.shape[0]
    by_swaps = tensor == 4 and groups == 2

    if by_swaps:
        half = head_rows // 2
        depth = half // CHUNKS
        plan = [(0, 0, head_rows)]
        for chunk in range(CHUNKS):
            plan += [(step, chunk * depth, depth) for step in (3, 2, 1)]
        cuts = cut(
            jnp.stack([group_index * half, tensor_index]), w_out, tuple(plan), share_cols
        )
        weights = [(cuts[0], 0, None)]
        for (step, start, _), sent in zip(plan[1:], cuts[1:]):
            arrived = swap(sent, "tensor", step)
            weights.append((arrived, step * head_rows + start, 0))
            weights.append((swap(arrived, "groups", 1), step * head_rows + start, 1))
    else:
        half = 0
        spread = lax.all_to_all(w_out, "tensor", 1, 0, tiled=True)
        weights = [(load(spread)[0], 0, None)]

    embeds = branch_embeds.reshape(dp, batches, per_block, depths, branch, feat_cols)
    gain = norm_gain.reshape(1, feat_cols)
    keyval = w_keyval.reshape(feat_cols, -1)
    w_query, keyval, embeds, cache_kv = load(w_query, keyval, embeds, cache_kv)
    places = jnp.stack([dp_index ^ step for step in range(dp)])
    info = jnp.concatenate(
        [
            places,
            jnp.stack([group_index * half, (1 - group_index) * half, tensor_index]),
        ]
    )
    if by_swaps:
        share_ids = jnp.stack([tensor_index ^ step for step in range(tensor)])
    else:
        share_ids = jnp.zeros((1,), jnp.int32)

    split = parents.reshape(dp, batches, per_block, depths - 1, branch)
    ordered = jnp.stack(
        [lax.dynamic_index_in_dim(split, dp_index ^ step, 0, False) for step in range(dp)]
    )
    slot = (
        jnp.arange(dp, dtype=jnp.int32)[:, None] * per_block
        + jnp.arange(per_block, dtype=jnp.int32)[None, :]
    )
    rows = dp * per_block * branch
    indices = []
    for level in range(depths):
        row = []
        for batch in range(batches):
            if level == 0:
                request = (
                    places[:, None] * local
                    + batch * per_block
                    + jnp.arange(per_block, dtype=jnp.int32)[None, :]
                )
                place = jnp.broadcast_to(request[:, :, None], (dp, per_block, branch))
            else:
                place = slot[:, :, None] * branch + ordered[:, batch, :, level - 1]
            row.append(place.reshape(rows, 1))
        indices.append(row)
    masks = tree_masks(ordered[0], depths, branch)

    earlier = [[] for _ in range(batches)]
    shares = [root_features] * batches
    gathered = [[root_features]] * batches
    held = None
    for level in range(depths):
        attended = []
        for batch in range(batches):
            sums = project(
                level,
                batch,
                share_ids,
                places,
                indices[level][batch],
                gathered[batch],
                embeds,
                gain,
                w_query,
                keyval,
            )
            parts = [sums[0]] + [swap(sums[step], "dp", step) for step in range(1, dp)]
            mixed, fresh = attend(
                batch,
                per_block,
                feat_cols * dp,
                head_cols,
                cache_lengths,
                parts,
                masks[level][batch],
                cache_kv,
                earlier[batch],
            )
            earlier[batch] = earlier[batch] + [fresh]
            if by_swaps:
                heads = [mixed] + [swap(mixed, "tensor", step) for step in range(1, tensor)]
                joined = jnp.concatenate(heads, axis=1)
            else:
                joined = lax.all_gather(mixed, "tensor", axis=1, tiled=True)
            attended.append([joined] + [swap(joined, "dp", step) for step in range(1, dp)])
        for batch in range(batches):
            shares[batch], *kept = output(
                level,
                batch,
                info,
                indices[level][batch],
                attended[batch],
                weights,
                shares[batch],
                embeds,
                share_cols,
            )
            if kept:
                weights = [(kept[0], 0, None)]
            held = store(
                level, batch, embeds.shape[:-1] + (share_cols,), info, shares[batch], held
            )
            if level + 1 == depths:
                continue
            own = shares[batch]
            if by_swaps:
                far = swap(own, "tensor", 3)
                gathered[batch] = [own, swap(own, "tensor", 1), swap(far, "tensor", 1), far]
            else:
                gathered[batch] = [lax.all_gather(own, "tensor", axis=1, tiled=True)]
    return held.reshape(requests, depths, branch, share_cols)


def solution(mesh):
    return jax.shard_map(
        shards,
        mesh=mesh,
        in_specs=(
            P("groups", "dp"),
            P("groups", None, None, "dp"),
            P("groups", None, None),
            P(("groups", "dp")),
            P(("groups", "dp"), None, None, "tensor"),
            P("dp"),
            P("dp", "tensor"),
            P("dp", None, "tensor"),
            P("tensor", "dp"),
        ),
        out_specs=P("groups", None, None, ("dp", "tensor")),
        check_vma=False,
    )
```

```python
import functools

import jax
import jax.numpy as jnp
from jax import lax
from jax.experimental import pallas as pl
from jax.experimental.pallas import tpu as pltpu
from jax.sharding import PartitionSpec as P

HD = 128
BATCHES = 1
CHUNKS = 2
EPSILON = 1e-05
MASKED = -1e30
LANES = 128
VMEM_BYTES = 20 * 1024 * 1024


def swap(x, axis, step):
    size = lax.axis_size(axis)
    return lax.ppermute(x, axis, [(i, i ^ step) for i in range(size)])


def parent_rows(chosen_ref, features):
    return jnp.dot(chosen_ref[...], features, preferred_element_type=jnp.float32)


def embed_rows(places_ref, embed_ref, batch, level, columns):
    dp, _, per_block = embed_ref.shape[:3]
    blocks = []
    for step in range(dp):
        for request in range(per_block):
            block = embed_ref[places_ref[step], batch, request, level, :, columns]
            blocks.append(block.astype(jnp.float32))
    return jnp.concatenate(blocks, axis=0)


def cut_kernel(plan, dp, info_ref, weight_ref, *refs):
    outs, sems = refs[:-1], refs[-1]
    share = outs[0].shape[1]
    copies = []
    for place, out_ref in enumerate(outs):
        step, start, depth = plan[place]
        row = start if step == 0 else pl.multiple_of(start + info_ref[dp], 16)
        column = pl.multiple_of((info_ref[dp + 2] ^ step) * share, LANES)
        copies.append(
            pltpu.make_async_copy(
                weight_ref.at[pl.ds(row, depth), pl.ds(column, share)],
                out_ref,
                sems.at[place],
            )
        )
    for copy in copies:
        copy.start()
    for copy in copies:
        copy.wait()


def cut(info, w_out, plan, share, dp):
    shapes = [(depth, share) for _, _, depth in plan]
    return pl.pallas_call(
        functools.partial(cut_kernel, plan, dp),
        grid_spec=pltpu.PrefetchScalarGridSpec(
            num_scalar_prefetch=1,
            grid=(1,),
            in_specs=[pl.BlockSpec(memory_space=pl.ANY)],
            out_specs=[pl.BlockSpec(memory_space=pl.ANY) for _ in shapes],
            scratch_shapes=[pltpu.SemaphoreType.DMA((len(shapes),))],
        ),
        out_shape=[jax.ShapeDtypeStruct(shape, w_out.dtype) for shape in shapes],
        compiler_params=pltpu.CompilerParams(vmem_limit_bytes=VMEM_BYTES),
        name="cut",
    )(info, w_out)


def load_kernel(parts, info_ref, source_ref, held_ref, sems):
    depth = source_ref.shape[0] // parts
    copies = [
        pltpu.make_async_copy(
            source_ref.at[pl.ds(part * depth, depth)],
            held_ref.at[pl.ds(part * depth, depth)],
            sems.at[part],
        )
        for part in range(parts)
    ]
    for copy in copies:
        copy.start()
    for copy in copies:
        copy.wait()


def load(info, x):
    parts = 4
    return pl.pallas_call(
        functools.partial(load_kernel, parts),
        in_specs=[pl.BlockSpec(memory_space=pltpu.SMEM), pl.BlockSpec(memory_space=pl.ANY)],
        out_specs=pl.BlockSpec(memory_space=pltpu.VMEM),
        out_shape=pltpu.VMEM(x.shape, x.dtype),
        scratch_shapes=[pltpu.SemaphoreType.DMA((parts,))],
        compiler_params=pltpu.CompilerParams(vmem_limit_bytes=VMEM_BYTES),
        name="load",
    )(info, x)


def prepare_kernel(batch, batches, dp, levels, branch, info_ref, parents_ref, *refs):
    root_ref, chosen_refs = refs[0], refs[1 : levels]
    mask_refs, table_ref = refs[levels : 2 * levels], refs[2 * levels]
    rows, requests = root_ref.shape
    local = requests // dp
    per_block = local // batches
    own = per_block * branch
    for level in range(levels):
        width = requests if level == 0 else rows
        line = lax.broadcasted_iota(jnp.int32, (branch, width), 0)
        column = lax.broadcasted_iota(jnp.int32, (branch, width), 1)
        for step in range(dp):
            for slot in range(per_block):
                request = info_ref[step] * local + batch * per_block + slot
                first = (step * per_block + slot) * branch
                if level == 0:
                    place = request
                else:
                    place = jnp.zeros((branch, width), jnp.int32)
                    for node in range(branch):
                        up = parents_ref[request, level - 1, node] + first
                        place = jnp.where(line == node, up, place)
                table_ref[first : first + branch, :width] = jnp.where(
                    column == place, 1.0, 0.0
                )
        chosen = table_ref[:, :width].astype(jnp.bfloat16)
        if level == 0:
            root_ref[...] = chosen
        else:
            chosen_refs[level - 1][...] = chosen
    ups = [ref[:own, :own] for ref in chosen_refs]
    line = lax.broadcasted_iota(jnp.int32, (own, own), 0)
    column = lax.broadcasted_iota(jnp.int32, (own, own), 1)
    for level in range(levels):
        current = jnp.where(line == column, 1.0, 0.0)
        blocks = [current]
        for upper in range(level, 0, -1):
            current = jnp.dot(
                current.astype(jnp.bfloat16), ups[upper - 1], preferred_element_type=jnp.float32
            )
            blocks.insert(0, current)
        for place in range(levels):
            span = slice(place * own, (place + 1) * own)
            if place < len(blocks):
                mask_refs[level][:, span] = blocks[place]
            else:
                mask_refs[level][:, span] = jnp.zeros((own, own), jnp.float32)


def prepare(batch, batches, info, parents, dp, levels, branch):
    requests = parents.shape[0]
    own = requests // dp // batches * branch
    rows = dp * own
    half, single = jnp.bfloat16, jnp.float32
    out_shape = [jax.ShapeDtypeStruct((rows, requests), half)]
    out_shape += [jax.ShapeDtypeStruct((rows, rows), half)] * (levels - 1)
    out_shape += [jax.ShapeDtypeStruct((own, levels * own), single)] * levels
    outs = pl.pallas_call(
        functools.partial(prepare_kernel, batch, batches, dp, levels, branch),
        in_specs=[pl.BlockSpec(memory_space=pltpu.SMEM)] * 2,
        out_specs=[pl.BlockSpec(memory_space=pltpu.VMEM)] * len(out_shape),
        out_shape=out_shape,
        scratch_shapes=[pltpu.VMEM((rows, max(rows, requests)), jnp.float32)],
        compiler_params=pltpu.CompilerParams(vmem_limit_bytes=VMEM_BYTES),
        name="prepare",
    )(info, parents)
    return outs[:levels], outs[levels:]


def project_kernel(level, batch, pieces, steps, dp, info_ref, index_ref, *refs):
    features = refs[:pieces]
    embed_ref, gain_ref, query_ref, keyval_ref = refs[pieces : pieces + 4]
    out_refs = refs[pieces + 4 : pieces + 4 + dp]
    cols = query_ref.shape[0] // steps
    query = keyval = squares = None
    for step in range(steps):
        offset = pl.multiple_of(info_ref[dp + 3 + step] * cols, LANES)
        columns = pl.ds(offset, cols)
        held = features[step][...] if pieces == steps else features[0][:, columns]
        state = parent_rows(index_ref, held) + embed_rows(
            info_ref, embed_ref, batch, level, columns
        )
        square = jnp.sum(state * state, axis=1, keepdims=True)
        gain = gain_ref[:, columns].astype(jnp.float32)
        scaled = (state * gain).astype(jnp.bfloat16)
        first = jnp.dot(scaled, query_ref[columns, :], preferred_element_type=jnp.float32)
        second = jnp.dot(scaled, keyval_ref[columns, :], preferred_element_type=jnp.float32)
        query = first if step == 0 else query + first
        keyval = second if step == 0 else keyval + second
        squares = square if step == 0 else squares + square
    head_cols = query.shape[1]
    width = head_cols + keyval.shape[1]
    rows = out_refs[0].shape[0]
    lane = lax.broadcasted_iota(jnp.int32, (rows, LANES), 1)
    for block in range(dp):
        span = slice(block * rows, (block + 1) * rows)
        high = squares[span].astype(jnp.bfloat16).astype(jnp.float32)
        low = squares[span] - high
        tail = jnp.where(lane == 0, high, jnp.where(lane == 1, low, 0.0))
        out_refs[block][:, :head_cols] = query[span].astype(jnp.bfloat16)
        out_refs[block][:, head_cols:width] = keyval[span].astype(jnp.bfloat16)
        out_refs[block][:, width:] = tail.astype(jnp.bfloat16)


def attend_kernel(
    dp, earlier, head_cols, model_width, base, branch, length_ref, *refs
):
    parts = refs[:dp]
    mask_ref, cache_ref = refs[dp : dp + 2]
    earlier_refs = refs[dp + 2 : dp + 2 + earlier]
    out_ref, fresh_ref = refs[dp + 2 + earlier :]
    total = parts[0][...].astype(jnp.float32)
    for part in parts[1:]:
        total = total + part[...].astype(jnp.float32)
    width = head_cols + fresh_ref.shape[1]
    squares = jnp.sum(total[:, width:], axis=1, keepdims=True)
    inv_rms = lax.rsqrt(squares / model_width + EPSILON)
    projected = (total[:, :width] * inv_rms).astype(jnp.bfloat16)
    fresh = projected[:, head_cols:]
    fresh_ref[...] = fresh
    _, _, cache, kv_cols = cache_ref.shape
    rows = total.shape[0]
    per_block = rows // branch
    kv_heads = kv_cols // HD
    group = head_cols // HD // kv_heads
    tree = [ref[...] for ref in earlier_refs] + [fresh]
    filler = mask_ref.shape[1] - rows * len(tree)
    tree += [jnp.zeros((filler, fresh.shape[1]), jnp.bfloat16)] if filler else []
    tree = jnp.concatenate(tree, axis=0)
    allowed = jnp.concatenate([mask_ref[...]] * group, axis=0) > 0.5
    column = lax.broadcasted_iota(jnp.int32, (branch, cache), 1)
    valid = [column < length_ref[base + request] for request in range(per_block)]
    across = (((1,), (1,)), ((), ()))
    scale = HD**-0.5
    for kv in range(kv_heads):
        first = kv * group
        queries = jnp.concatenate(
            [projected[:, (first + g) * HD : (first + g + 1) * HD] for g in range(group)], axis=0
        )
        key_cols = slice(kv * HD, (kv + 1) * HD)
        value_cols = slice(kv_cols + kv * HD, kv_cols + (kv + 1) * HD)
        far = lax.dot_general(
            queries, tree[:, key_cols], across, preferred_element_type=jnp.float32
        )
        far = jnp.where(allowed, far * scale, MASKED)
        found = []
        for request in range(per_block):
            keys = cache_ref[base + request, 0, :, key_cols]
            scores = lax.dot_general(queries, keys, across, preferred_element_type=jnp.float32)
            found.append(scores)
        blocks = []
        for g in range(group):
            for request in range(per_block):
                start = g * rows + request * branch
                block = found[request][start : start + branch] * scale
                blocks.append(jnp.where(valid[request], block, MASKED))
        near = jnp.concatenate(blocks, axis=0)
        top = jnp.maximum(
            jnp.max(near, axis=1, keepdims=True), jnp.max(far, axis=1, keepdims=True)
        )
        near = jnp.exp(near - top)
        far = jnp.exp(far - top)
        below = jnp.sum(near, axis=1, keepdims=True) + jnp.sum(far, axis=1, keepdims=True)
        near = (near / below).astype(jnp.bfloat16)
        far = (far / below).astype(jnp.bfloat16)
        mixed = jnp.dot(far, tree[:, value_cols], preferred_element_type=jnp.float32)
        found = []
        for request in range(per_block):
            values = cache_ref[base + request, 1, :, key_cols]
            found.append(jnp.dot(near, values, preferred_element_type=jnp.float32))
        for g in range(group):
            blocks = []
            for request in range(per_block):
                start = g * rows + request * branch
                blocks.append(
                    found[request][start : start + branch] + mixed[start : start + branch]
                )
            block = jnp.concatenate(blocks, axis=0).astype(jnp.bfloat16)
            out_ref[:, (first + g) * HD : (first + g + 1) * HD] = block


def output_kernel(level, batch, dp, weights, keep, info_ref, index_ref, *refs):
    attended = refs[:dp]
    weight_refs = refs[dp : dp + len(weights)]
    feature_ref, embed_ref = refs[dp + len(weights) : dp + len(weights) + 2]
    rest = refs[dp + len(weights) + 2 :]
    fresh_ref, gathered_ref = rest[0], rest[-1]
    rows = attended[0].shape[0]
    share = fresh_ref.shape[1]
    for step in range(dp):
        gathered_ref[step * rows : (step + 1) * rows, :] = attended[step][...]
    spans = []
    for weight_ref, (start, side) in zip(weight_refs, weights):
        depth = weight_ref.shape[0]
        if side is not None:
            start = pl.multiple_of(start + info_ref[dp + side], LANES)
        spans.append(pl.ds(start, depth))
        if keep:
            rest[1][spans[-1], :] = weight_ref[...]
    if keep:
        weight_refs, spans = [rest[1]], [slice(None)]
    offset = pl.multiple_of(info_ref[dp + 2] * share, LANES)
    block = min(2 * LANES, share)
    for start in range(0, share, block):
        if feature_ref.shape[1] == share:
            held = feature_ref[:, start : start + block]
        else:
            held = feature_ref[:, pl.ds(offset + start, block)]
        fresh = parent_rows(index_ref, held) + embed_rows(
            info_ref, embed_ref, batch, level, pl.ds(offset + start, block)
        )
        for weight_ref, span in zip(weight_refs, spans):
            fresh = fresh + jnp.dot(
                gathered_ref[:, span],
                weight_ref[:, start : start + block],
                preferred_element_type=jnp.float32,
            )
        fresh_ref[:, start : start + block] = fresh.astype(jnp.bfloat16)


def store_kernel(info_ref, fresh_ref, *refs):
    out_ref = refs[-1]
    dp, per_block, branch = out_ref.shape[0], out_ref.shape[2], out_ref.shape[4]
    fresh = fresh_ref[...].astype(jnp.float32)
    for step in range(dp):
        for request in range(per_block):
            start = (step * per_block + request) * branch
            block = fresh[start : start + branch].astype(jnp.bfloat16)
            out_ref[info_ref[step], 0, request, 0] = block


def full(x):
    return pl.BlockSpec(x.shape, lambda i, *_: (0,) * x.ndim)


def project(level, batch, steps, info, index, pieces, embeds, gain, w_query, keyval):
    dp, _, per_block, _, branch, feat_cols = embeds.shape
    head_cols, kv_cols = w_query.shape[1], keyval.shape[1]
    rows = per_block * branch
    width = head_cols + kv_cols + LANES
    operands = [index, *pieces, embeds, gain, w_query, keyval]
    return pl.pallas_call(
        functools.partial(project_kernel, level, batch, len(pieces), steps, dp),
        grid_spec=pltpu.PrefetchScalarGridSpec(
            num_scalar_prefetch=1,
            grid=(),
            in_specs=[pl.BlockSpec(memory_space=pltpu.VMEM)] * len(operands),
            out_specs=[pl.BlockSpec(memory_space=pltpu.VMEM)] * dp,
        ),
        out_shape=[jax.ShapeDtypeStruct((rows, width), jnp.bfloat16)] * dp,
        compiler_params=pltpu.CompilerParams(vmem_limit_bytes=VMEM_BYTES),
        cost_estimate=pl.CostEstimate(
            flops=2 * dp * rows * feat_cols * (head_cols + kv_cols),
            bytes_accessed=4 * dp * rows * feat_cols,
            transcendentals=0,
        ),
        name="project",
    )(info, *operands)


def attend(batch, per_block, model_width, head_cols, lengths, parts, mask, cache, earlier):
    rows, width = parts[0].shape
    fresh_cols = width - LANES - head_cols
    operands = [*parts, mask, cache, *earlier]
    return pl.pallas_call(
        functools.partial(
            attend_kernel,
            len(parts),
            len(earlier),
            head_cols,
            model_width,
            batch * per_block,
            rows // per_block,
        ),
        grid_spec=pltpu.PrefetchScalarGridSpec(
            num_scalar_prefetch=1,
            grid=(),
            in_specs=[pl.BlockSpec(memory_space=pltpu.VMEM)] * len(operands),
            out_specs=[pl.BlockSpec(memory_space=pltpu.VMEM)] * 2,
        ),
        out_shape=[
            jax.ShapeDtypeStruct((rows, head_cols), jnp.bfloat16),
            jax.ShapeDtypeStruct((rows, fresh_cols), jnp.bfloat16),
        ],
        compiler_params=pltpu.CompilerParams(vmem_limit_bytes=VMEM_BYTES),
        cost_estimate=pl.CostEstimate(
            flops=4 * rows * head_cols * cache.shape[2],
            bytes_accessed=4 * cache.shape[2] * per_block * HD,
            transcendentals=rows * head_cols * 4,
        ),
        name="attend",
    )(lengths, *operands)


def output(level, batch, info, index, attended, weights, features, embeds, share_cols):
    dp, _, per_block, _, branch, _ = embeds.shape
    rows = dp * per_block * branch
    arrays = [w for w, _, _ in weights]
    places = [(start, side) for _, start, side in weights]
    depth = sum(w.shape[0] for w in arrays)
    keep = len(weights) > 1
    operands = [index, *attended, *arrays, features, embeds]
    out_shape = [jax.ShapeDtypeStruct((rows, share_cols), jnp.bfloat16)]
    if keep:
        out_shape.append(pltpu.VMEM((depth, share_cols), jnp.bfloat16))
    return pl.pallas_call(
        functools.partial(output_kernel, level, batch, dp, places, keep),
        grid_spec=pltpu.PrefetchScalarGridSpec(
            num_scalar_prefetch=1,
            grid=(),
            in_specs=[pl.BlockSpec(memory_space=pltpu.VMEM)] * len(operands),
            out_specs=[pl.BlockSpec(memory_space=pltpu.VMEM)] * len(out_shape),
            scratch_shapes=[pltpu.VMEM((rows, depth), jnp.bfloat16)],
        ),
        out_shape=out_shape,
        compiler_params=pltpu.CompilerParams(vmem_limit_bytes=VMEM_BYTES),
        cost_estimate=pl.CostEstimate(
            flops=2 * rows * depth * share_cols,
            bytes_accessed=2 * rows * depth,
            transcendentals=0,
        ),
        name="output",
    )(info, *operands)


def store(level, batch, shape, info, fresh, held):
    dp, _, per_block, _, branch, share_cols = shape
    operands = [info, fresh]
    in_specs = [full(fresh)]
    aliases = {}
    if held is not None:
        in_specs.append(pl.BlockSpec(memory_space=pl.ANY))
        aliases = {2: 0}
        operands.append(held)
    return pl.pallas_call(
        store_kernel,
        grid_spec=pltpu.PrefetchScalarGridSpec(
            num_scalar_prefetch=1,
            grid=(1,),
            in_specs=in_specs,
            out_specs=pl.BlockSpec(
                (dp, 1, per_block, 1, branch, share_cols),
                lambda i, s: (0, batch, 0, level, 0, 0),
            ),
        ),
        out_shape=jax.ShapeDtypeStruct(shape, jnp.bfloat16),
        input_output_aliases=aliases,
        compiler_params=pltpu.CompilerParams(vmem_limit_bytes=VMEM_BYTES),
        cost_estimate=pl.CostEstimate(
            flops=0, bytes_accessed=4 * fresh.size, transcendentals=0
        ),
        name="store",
    )(*operands)


def shards(
    root_features,
    branch_embeds,
    parents,
    cache_lengths,
    cache_kv,
    norm_gain,
    w_query,
    w_keyval,
    w_out,
):
    requests, depths, branch, feat_cols = branch_embeds.shape
    dp, tensor, groups = (lax.axis_size(name) for name in ("dp", "tensor", "groups"))
    dp_index, tensor_index, group_index = (
        lax.axis_index(name).astype(jnp.int32) for name in ("dp", "tensor", "groups")
    )
    local = requests // dp
    batches = BATCHES
    per_block = local // batches
    share_cols = feat_cols // tensor
    head_cols = w_query.shape[1]
    head_rows = w_out.shape[0]
    by_swaps = tensor == 4 and groups == 2

    half = head_rows // 2 if by_swaps else 0
    steps = tensor if by_swaps else 1
    info = [dp_index ^ step for step in range(dp)]
    info += [group_index * half, (1 - group_index) * half, tensor_index]
    info += [tensor_index ^ step for step in range(tensor)] if by_swaps else [0 * dp_index]
    info = jnp.stack(info)

    if by_swaps:
        depth = half // CHUNKS
        plan = [(0, 0, head_rows)]
        for chunk in range(CHUNKS):
            plan += [(step, chunk * depth, depth) for step in (3, 2, 1)]
        cuts = cut(info, w_out, tuple(plan), share_cols, dp)
        weights = [(cuts[0], 0, None)]
        for (step, start, _), sent in zip(plan[1:], cuts[1:]):
            arrived = swap(sent, "tensor", step)
            weights.append((arrived, step * head_rows + start, 0))
            weights.append((swap(arrived, "groups", 1), step * head_rows + start, 1))
    else:
        spread = lax.all_to_all(w_out, "tensor", 1, 0, tiled=True)
        weights = [(load(info, spread), 0, None)]

    chosen, masks = [], []
    for batch in range(batches):
        made = prepare(batch, batches, info, parents, dp, depths, branch)
        chosen.append(made[0])
        masks.append(made[1])
    embeds = branch_embeds.reshape(dp, batches, per_block, depths, branch, feat_cols)
    gain = norm_gain.reshape(1, feat_cols)
    keyval = w_keyval.reshape(feat_cols, -1)
    w_query, keyval, embeds, cache_kv = (
        load(info, x) for x in (w_query, keyval, embeds, cache_kv)
    )

    earlier = [[] for _ in range(batches)]
    shares = [root_features] * batches
    gathered = [[root_features]] * batches
    held = None
    for level in range(depths):
        attended = []
        for batch in range(batches):
            sums = project(
                level,
                batch,
                steps,
                info,
                chosen[batch][level],
                gathered[batch],
                embeds,
                gain,
                w_query,
                keyval,
            )
            parts = [sums[0]] + [swap(sums[step], "dp", step) for step in range(1, dp)]
            mixed, fresh = attend(
                batch,
                per_block,
                feat_cols * dp,
                head_cols,
                cache_lengths,
                parts,
                masks[batch][level],
                cache_kv,
                earlier[batch],
            )
            earlier[batch] = earlier[batch] + [fresh]
            if by_swaps:
                heads = [mixed] + [swap(mixed, "tensor", step) for step in range(1, tensor)]
                joined = jnp.concatenate(heads, axis=1)
            else:
                joined = lax.all_gather(mixed, "tensor", axis=1, tiled=True)
            attended.append([joined] + [swap(joined, "dp", step) for step in range(1, dp)])
        for batch in range(batches):
            shares[batch], *kept = output(
                level,
                batch,
                info,
                chosen[batch][level],
                attended[batch],
                weights,
                shares[batch],
                embeds,
                share_cols,
            )
            if kept:
                weights = [(kept[0], 0, None)]
            held = store(
                level, batch, embeds.shape[:-1] + (share_cols,), info, shares[batch], held
            )
            if level + 1 == depths:
                continue
            own = shares[batch]
            if by_swaps:
                far = swap(own, "tensor", 3)
                gathered[batch] = [own, swap(own, "tensor", 1), swap(far, "tensor", 1), far]
            else:
                gathered[batch] = [lax.all_gather(own, "tensor", axis=1, tiled=True)]
    return held.reshape(requests, depths, branch, share_cols)


def solution(mesh):
    return jax.shard_map(
        shards,
        mesh=mesh,
        in_specs=(
            P("groups", "dp"),
            P("groups", None, None, "dp"),
            P("groups", None, None),
            P(("groups", "dp")),
            P(("groups", "dp"), None, None, "tensor"),
            P("dp"),
            P("dp", "tensor"),
            P("dp", None, "tensor"),
            P("tensor", "dp"),
        ),
        out_specs=P("groups", None, None, ("dp", "tensor")),
        check_vma=False,
    )
```

```python
import functools

import jax
import jax.numpy as jnp
from jax import lax
from jax.experimental import pallas as pl
from jax.experimental.pallas import tpu as pltpu
from jax.sharding import PartitionSpec as P

HD = 128
BATCHES = 1
EPSILON = 1e-05
MASKED = -1e30
LANES = 128
VMEM_BYTES = 20 * 1024 * 1024


def swap(x, axis, step):
    size = lax.axis_size(axis)
    return lax.ppermute(x, axis, [(i, i ^ step) for i in range(size)])


def parent_rows(chosen_ref, features):
    return jnp.dot(chosen_ref[...], features, preferred_element_type=jnp.float32)


def embed_rows(places_ref, embed_ref, batch, level, columns):
    dp, _, per_block = embed_ref.shape[:3]
    blocks = []
    for step in range(dp):
        for request in range(per_block):
            block = embed_ref[places_ref[step], batch, request, level, :, columns]
            blocks.append(block.astype(jnp.float32))
    return jnp.concatenate(blocks, axis=0)


def cut_kernel(plan, dp, info_ref, weight_ref, *refs):
    outs, sems = refs[:-1], refs[-1]
    share = outs[0].shape[1]
    copies = []
    for place, out_ref in enumerate(outs):
        step, start, depth = plan[place]
        row = start if step == 0 else pl.multiple_of(start + info_ref[dp], 16)
        column = pl.multiple_of((info_ref[dp + 2] ^ step) * share, LANES)
        copies.append(
            pltpu.make_async_copy(
                weight_ref.at[pl.ds(row, depth), pl.ds(column, share)],
                out_ref,
                sems.at[place],
            )
        )
    for copy in copies:
        copy.start()
    for copy in copies:
        copy.wait()


def cut(info, w_out, plan, share, dp):
    shapes = [(depth, share) for _, _, depth in plan]
    return pl.pallas_call(
        functools.partial(cut_kernel, plan, dp),
        grid_spec=pltpu.PrefetchScalarGridSpec(
            num_scalar_prefetch=1,
            grid=(1,),
            in_specs=[pl.BlockSpec(memory_space=pltpu.HBM)],
            out_specs=[pl.BlockSpec(memory_space=pl.ANY) for _ in shapes],
            scratch_shapes=[pltpu.SemaphoreType.DMA((len(shapes),))],
        ),
        out_shape=[jax.ShapeDtypeStruct(shape, w_out.dtype) for shape in shapes],
        compiler_params=pltpu.CompilerParams(vmem_limit_bytes=VMEM_BYTES),
        name="cut",
    )(info, w_out)


def load_kernel(parts, info_ref, source_ref, held_ref, sems):
    depth = source_ref.shape[0] // parts
    copies = [
        pltpu.make_async_copy(
            source_ref.at[pl.ds(part * depth, depth)],
            held_ref.at[pl.ds(part * depth, depth)],
            sems.at[part],
        )
        for part in range(parts)
    ]
    for copy in copies:
        copy.start()
    for copy in copies:
        copy.wait()


def load(info, x):
    parts = 4
    return pl.pallas_call(
        functools.partial(load_kernel, parts),
        in_specs=[pl.BlockSpec(memory_space=pltpu.SMEM), pl.BlockSpec(memory_space=pl.ANY)],
        out_specs=pl.BlockSpec(memory_space=pltpu.VMEM),
        out_shape=pltpu.VMEM(x.shape, x.dtype),
        scratch_shapes=[pltpu.SemaphoreType.DMA((parts,))],
        compiler_params=pltpu.CompilerParams(vmem_limit_bytes=VMEM_BYTES),
        name="load",
    )(info, x)


def prepare_kernel(batch, batches, dp, levels, branch, info_ref, parents_ref, *refs):
    count = len(levels)
    chosen_refs, mask_refs, table_ref = refs[:count], refs[count : 2 * count], refs[-1]
    rows, requests = table_ref.shape[0], parents_ref.shape[0]
    local = requests // dp
    per_block = local // batches
    own = per_block * branch
    for chosen_ref, level in zip(chosen_refs, levels):
        width = chosen_ref.shape[1]
        line = lax.broadcasted_iota(jnp.int32, (branch, width), 0)
        column = lax.broadcasted_iota(jnp.int32, (branch, width), 1)
        for step in range(dp):
            for slot in range(per_block):
                request = info_ref[step] * local + batch * per_block + slot
                first = (step * per_block + slot) * branch
                if level == 0:
                    place = request
                else:
                    place = jnp.zeros((branch, width), jnp.int32)
                    for node in range(branch):
                        up = parents_ref[request, level - 1, node] + first
                        place = jnp.where(line == node, up, place)
                table_ref[first : first + branch, :width] = jnp.where(
                    column == place, 1.0, 0.0
                )
        chosen_ref[...] = table_ref[:, :width].astype(jnp.bfloat16)
    line = lax.broadcasted_iota(jnp.int32, (own, own), 0)
    column = lax.broadcasted_iota(jnp.int32, (own, own), 1)
    for mask_ref, level in zip(mask_refs, levels):
        current = jnp.where(line == column, 1.0, 0.0)
        blocks = [current]
        for upper in range(level, 0, -1):
            above = chosen_refs[upper - levels[0]][:own, :own]
            current = jnp.dot(
                current.astype(jnp.bfloat16), above, preferred_element_type=jnp.float32
            )
            blocks.insert(0, current)
        for place in range(mask_ref.shape[1] // own):
            span = slice(place * own, (place + 1) * own)
            if place < len(blocks):
                mask_ref[:, span] = blocks[place]
            else:
                mask_ref[:, span] = jnp.zeros((own, own), jnp.float32)


def prepare(batch, batches, info, parents, dp, levels, depths, branch):
    requests = parents.shape[0]
    own = requests // dp // batches * branch
    rows = dp * own
    out_shape = [
        jax.ShapeDtypeStruct((rows, rows if level else requests), jnp.bfloat16)
        for level in levels
    ]
    out_shape += [jax.ShapeDtypeStruct((own, depths * own), jnp.float32) for _ in levels]
    outs = pl.pallas_call(
        functools.partial(prepare_kernel, batch, batches, dp, levels, branch),
        in_specs=[pl.BlockSpec(memory_space=pltpu.SMEM)] * 2,
        out_specs=[pl.BlockSpec(memory_space=pltpu.VMEM)] * len(out_shape),
        out_shape=out_shape,
        scratch_shapes=[pltpu.VMEM((rows, max(rows, requests)), jnp.float32)],
        compiler_params=pltpu.CompilerParams(vmem_limit_bytes=VMEM_BYTES),
        name="prepare",
    )(info, parents)
    return list(outs[: len(levels)]), list(outs[len(levels) :])


def project_kernel(
    level, batch, places, share, spread, last, dp, info_ref, index_ref, *refs
):
    pieces = len(places) if spread else 1
    features = refs[:pieces]
    embed_ref, gain_ref, query_ref, keyval_ref = refs[pieces : pieces + 4]
    rest = refs[pieces + 4 :]
    head_cols = query_ref.shape[1]
    width = head_cols + keyval_ref.shape[1]
    query = keyval = squares = None
    for piece, place in enumerate(places):
        place, start = place
        cols = features[piece].shape[1] if spread else share
        offset = pl.multiple_of(info_ref[dp + 3 + place] * share + start, LANES)
        columns = pl.ds(offset, cols)
        held = features[piece][...] if spread else features[0][:, columns]
        state = parent_rows(index_ref, held) + embed_rows(
            info_ref, embed_ref, batch, level, columns
        )
        square = jnp.sum(state * state, axis=1, keepdims=True)
        gain = gain_ref[:, columns].astype(jnp.float32)
        scaled = (state * gain).astype(jnp.bfloat16)
        first = jnp.dot(scaled, query_ref[columns, :], preferred_element_type=jnp.float32)
        second = jnp.dot(scaled, keyval_ref[columns, :], preferred_element_type=jnp.float32)
        query = first if piece == 0 else query + first
        keyval = second if piece == 0 else keyval + second
        squares = square if piece == 0 else squares + square
    if len(rest) != (dp if last else 1):
        before_ref = rest[0]
        rest = rest[1:]
        query = query + before_ref[:, :head_cols]
        keyval = keyval + before_ref[:, head_cols:width]
        squares = squares + before_ref[:, width : width + 1]
    if not last:
        total_ref = rest[0]
        total_ref[:, :head_cols] = query
        total_ref[:, head_cols:width] = keyval
        total_ref[:, width:] = jnp.broadcast_to(squares, (squares.shape[0], LANES))
        return
    out_refs = rest
    rows = out_refs[0].shape[0]
    lane = lax.broadcasted_iota(jnp.int32, (rows, LANES), 1)
    for block in range(dp):
        span = slice(block * rows, (block + 1) * rows)
        high = squares[span].astype(jnp.bfloat16).astype(jnp.float32)
        low = squares[span] - high
        tail = jnp.where(lane == 0, high, jnp.where(lane == 1, low, 0.0))
        out_refs[block][:, :head_cols] = query[span].astype(jnp.bfloat16)
        out_refs[block][:, head_cols:width] = keyval[span].astype(jnp.bfloat16)
        out_refs[block][:, width:] = tail.astype(jnp.bfloat16)


def attend_kernel(
    dp, earlier, head_cols, model_width, base, branch, length_ref, *refs
):
    parts = refs[:dp]
    mask_ref, cache_ref = refs[dp : dp + 2]
    earlier_refs = refs[dp + 2 : dp + 2 + earlier]
    out_ref, fresh_ref = refs[dp + 2 + earlier :]
    total = parts[0][...].astype(jnp.float32)
    for part in parts[1:]:
        total = total + part[...].astype(jnp.float32)
    width = head_cols + fresh_ref.shape[1]
    squares = jnp.sum(total[:, width:], axis=1, keepdims=True)
    inv_rms = lax.rsqrt(squares / model_width + EPSILON)
    projected = (total[:, :width] * inv_rms).astype(jnp.bfloat16)
    fresh = projected[:, head_cols:]
    fresh_ref[...] = fresh
    _, _, cache, kv_cols = cache_ref.shape
    rows = total.shape[0]
    per_block = rows // branch
    kv_heads = kv_cols // HD
    group = head_cols // HD // kv_heads
    tree = [ref[...] for ref in earlier_refs] + [fresh]
    filler = mask_ref.shape[1] - rows * len(tree)
    tree += [jnp.zeros((filler, fresh.shape[1]), jnp.bfloat16)] if filler else []
    tree = jnp.concatenate(tree, axis=0)
    allowed = jnp.concatenate([mask_ref[...]] * group, axis=0) > 0.5
    column = lax.broadcasted_iota(jnp.int32, (branch, cache), 1)
    valid = [column < length_ref[base + request] for request in range(per_block)]
    across = (((1,), (1,)), ((), ()))
    scale = HD**-0.5
    for kv in range(kv_heads):
        first = kv * group
        queries = jnp.concatenate(
            [projected[:, (first + g) * HD : (first + g + 1) * HD] for g in range(group)], axis=0
        )
        key_cols = slice(kv * HD, (kv + 1) * HD)
        value_cols = slice(kv_cols + kv * HD, kv_cols + (kv + 1) * HD)
        far = lax.dot_general(
            queries, tree[:, key_cols], across, preferred_element_type=jnp.float32
        )
        far = jnp.where(allowed, far * scale, MASKED)
        found = []
        for request in range(per_block):
            keys = cache_ref[base + request, 0, :, key_cols]
            scores = lax.dot_general(queries, keys, across, preferred_element_type=jnp.float32)
            found.append(scores)
        blocks = []
        for g in range(group):
            for request in range(per_block):
                start = g * rows + request * branch
                block = found[request][start : start + branch] * scale
                blocks.append(jnp.where(valid[request], block, MASKED))
        near = jnp.concatenate(blocks, axis=0)
        top = jnp.maximum(
            jnp.max(near, axis=1, keepdims=True), jnp.max(far, axis=1, keepdims=True)
        )
        near = jnp.exp(near - top)
        far = jnp.exp(far - top)
        below = jnp.sum(near, axis=1, keepdims=True) + jnp.sum(far, axis=1, keepdims=True)
        near = (near / below).astype(jnp.bfloat16)
        far = (far / below).astype(jnp.bfloat16)
        mixed = jnp.dot(far, tree[:, value_cols], preferred_element_type=jnp.float32)
        found = []
        for request in range(per_block):
            values = cache_ref[base + request, 1, :, key_cols]
            found.append(jnp.dot(near, values, preferred_element_type=jnp.float32))
        for g in range(group):
            blocks = []
            for request in range(per_block):
                start = g * rows + request * branch
                blocks.append(
                    found[request][start : start + branch] + mixed[start : start + branch]
                )
            block = jnp.concatenate(blocks, axis=0).astype(jnp.bfloat16)
            out_ref[:, (first + g) * HD : (first + g + 1) * HD] = block


def output_kernel(level, batch, dp, weights, keep, final, info_ref, index_ref, *refs):
    attended = refs[:dp]
    weight_refs = refs[dp : dp + len(weights)]
    feature_ref, embed_ref = refs[dp + len(weights) : dp + len(weights) + 2]
    rest = refs[dp + len(weights) + 2 :]
    rows = attended[0].shape[0]
    if final:
        _, held_ref, gathered_ref, staged_ref, sems = rest
        share = staged_ref.shape[3]
    else:
        kept, gathered_ref = rest[-2], rest[-1]
        out_refs = rest[:-2] if keep else rest[:-1]
        share = out_refs[0].shape[1]
    for step in range(dp):
        gathered_ref[step * rows : (step + 1) * rows, :] = attended[step][...]
    spans = []
    for weight_ref, (start, side) in zip(weight_refs, weights):
        depth = weight_ref.shape[0]
        if side is not None:
            start = pl.multiple_of(start + info_ref[dp + side], LANES // 4)
        spans.append(pl.ds(start, depth))
        if keep:
            kept[spans[-1], :] = weight_ref[...]
    if keep:
        weight_refs = [kept]
    offset = pl.multiple_of(info_ref[dp + 2] * share, LANES)
    block = min(2 * LANES, share)
    for start in range(0, share, block):
        if feature_ref.shape[1] == share:
            held = feature_ref[:, start : start + block]
        else:
            held = feature_ref[:, pl.ds(offset + start, block)]
        fresh = parent_rows(index_ref, held) + embed_rows(
            info_ref, embed_ref, batch, level, pl.ds(offset + start, block)
        )
        fresh = fresh + jnp.dot(
            gathered_ref[...],
            weight_refs[0][:, start : start + block],
            preferred_element_type=jnp.float32,
        )
        if not final:
            write_halves(fresh.astype(jnp.bfloat16), start, out_refs)
            continue
        branch = staged_ref.shape[2]
        for step in range(dp):
            for request in range(staged_ref.shape[1]):
                first = (step * staged_ref.shape[1] + request) * branch
                staged_ref[step, request, :, start : start + block] = fresh[
                    first : first + branch
                ].astype(jnp.bfloat16)
    if final:
        copies = [
            pltpu.make_async_copy(
                staged_ref.at[step],
                held_ref.at[info_ref[step], batch, :, level],
                sems.at[step],
            )
            for step in range(dp)
        ]
        for copy in copies:
            copy.start()
        for copy in copies:
            copy.wait()


def store_kernel(info_ref, fresh_ref, *refs):
    out_ref = refs[-1]
    dp, per_block, branch = out_ref.shape[0], out_ref.shape[2], out_ref.shape[4]
    fresh = fresh_ref[...].astype(jnp.float32)
    for step in range(dp):
        for request in range(per_block):
            start = (step * per_block + request) * branch
            block = fresh[start : start + branch].astype(jnp.bfloat16)
            out_ref[info_ref[step], 0, request, 0] = block


def partial_kernel(dp, info_ref, *refs):
    attended, weight_ref = refs[:dp], refs[dp]
    outs = refs[dp + 1 :]
    left = jnp.concatenate([ref[...] for ref in attended], axis=0)
    share = outs[0].shape[1]
    block = min(4 * LANES, share)
    for place, out_ref in enumerate(outs):
        offset = pl.multiple_of(info_ref[dp + 3 + place] * share, LANES)
        for start in range(0, share, block):
            out_ref[:, start : start + block] = jnp.dot(
                left,
                weight_ref[:, pl.ds(offset + start, block)],
                preferred_element_type=jnp.float32,
            ).astype(jnp.bfloat16)


def partial(info, attended, w_out, shares):
    dp = len(attended)
    rows = dp * attended[0].shape[0]
    share_cols = w_out.shape[1] // shares
    operands = [*attended, w_out]
    return pl.pallas_call(
        functools.partial(partial_kernel, dp),
        grid_spec=pltpu.PrefetchScalarGridSpec(
            num_scalar_prefetch=1,
            grid=(),
            in_specs=[pl.BlockSpec(memory_space=pltpu.VMEM)] * len(operands),
            out_specs=[pl.BlockSpec(memory_space=pltpu.VMEM)] * shares,
        ),
        out_shape=[jax.ShapeDtypeStruct((rows, share_cols), jnp.bfloat16)] * shares,
        compiler_params=pltpu.CompilerParams(vmem_limit_bytes=VMEM_BYTES),
        name="partial",
    )(info, *operands)


def combine_kernel(level, batch, dp, info_ref, index_ref, *refs):
    terms, (feature_ref, embed_ref, *out_refs) = refs[:-5], refs[-5:]
    share = out_refs[0].shape[1]
    offset = pl.multiple_of(info_ref[dp + 2] * share, LANES)
    columns = pl.ds(offset, share)
    fresh = parent_rows(index_ref, feature_ref[:, columns]) + embed_rows(
        info_ref, embed_ref, batch, level, columns
    )
    for term in terms:
        fresh = fresh + term[...].astype(jnp.float32)
    write_halves(fresh.astype(jnp.bfloat16), 0, out_refs)


def write_halves(fresh, start, out_refs):
    width = fresh.shape[1]
    out_refs[0][:, start : start + width] = fresh
    for half_ref in out_refs[1:]:
        half = half_ref.shape[1]
        low, high = max(start, 0), min(start + width, half)
        if low < high:
            half_ref[:, low:high] = fresh[:, low - start : high - start]
        start -= half


def halves(rows, share_cols):
    shapes = [(rows, share_cols), (rows, share_cols // 2), (rows, share_cols // 2)]
    return [jax.ShapeDtypeStruct(shape, jnp.bfloat16) for shape in shapes]


def combine(level, batch, info, index, terms, features, embeds):
    operands = [index, *terms, features, embeds]
    return pl.pallas_call(
        functools.partial(combine_kernel, level, batch, embeds.shape[0]),
        grid_spec=pltpu.PrefetchScalarGridSpec(
            num_scalar_prefetch=1,
            grid=(),
            in_specs=[pl.BlockSpec(memory_space=pltpu.VMEM)] * len(operands),
            out_specs=[pl.BlockSpec(memory_space=pltpu.VMEM)] * 3,
        ),
        out_shape=halves(*terms[0].shape),
        compiler_params=pltpu.CompilerParams(vmem_limit_bytes=VMEM_BYTES),
        name="combine",
    )(info, *operands)


def store_kernel(info_ref, fresh_ref, *refs):
    out_ref = refs[-1]
    dp, per_block, branch = out_ref.shape[0], out_ref.shape[2], out_ref.shape[4]
    fresh = fresh_ref[...].astype(jnp.float32)
    for step in range(dp):
        for request in range(per_block):
            start = (step * per_block + request) * branch
            block = fresh[start : start + branch].astype(jnp.bfloat16)
            out_ref[info_ref[step], 0, request, 0] = block


def full(x):
    return pl.BlockSpec(x.shape, lambda i, *_: (0,) * x.ndim)


def project(
    level, batch, places, share, info, index, pieces, embeds, gain, w_query, keyval, before, last
):
    dp, _, per_block, _, branch, feat_cols = embeds.shape
    head_cols, kv_cols = w_query.shape[1], keyval.shape[1]
    rows = per_block * branch
    width = head_cols + kv_cols + LANES
    operands = [index, *pieces, embeds, gain, w_query, keyval]
    operands += [] if before is None else [before]
    if last:
        out_shape = [jax.ShapeDtypeStruct((rows, width), jnp.bfloat16)] * dp
    else:
        out_shape = [jax.ShapeDtypeStruct((dp * rows, width), jnp.float32)]
    spread = level > 0 and len(pieces) == len(places)
    return pl.pallas_call(
        functools.partial(project_kernel, level, batch, places, share, spread, last, dp),
        grid_spec=pltpu.PrefetchScalarGridSpec(
            num_scalar_prefetch=1,
            grid=(),
            in_specs=[pl.BlockSpec(memory_space=pltpu.VMEM)] * len(operands),
            out_specs=[pl.BlockSpec(memory_space=pltpu.VMEM)] * len(out_shape),
        ),
        out_shape=out_shape,
        compiler_params=pltpu.CompilerParams(vmem_limit_bytes=VMEM_BYTES),
        cost_estimate=pl.CostEstimate(
            flops=2 * dp * rows * feat_cols * (head_cols + kv_cols),
            bytes_accessed=4 * dp * rows * feat_cols,
            transcendentals=0,
        ),
        name="project",
    )(info, *operands)


def attend(batch, per_block, model_width, head_cols, lengths, parts, mask, cache, earlier):
    rows, width = parts[0].shape
    fresh_cols = width - LANES - head_cols
    operands = [*parts, mask, cache, *earlier]
    return pl.pallas_call(
        functools.partial(
            attend_kernel,
            len(parts),
            len(earlier),
            head_cols,
            model_width,
            batch * per_block,
            rows // per_block,
        ),
        grid_spec=pltpu.PrefetchScalarGridSpec(
            num_scalar_prefetch=1,
            grid=(),
            in_specs=[pl.BlockSpec(memory_space=pltpu.VMEM)] * len(operands),
            out_specs=[pl.BlockSpec(memory_space=pltpu.VMEM)] * 2,
        ),
        out_shape=[
            jax.ShapeDtypeStruct((rows, head_cols), jnp.bfloat16),
            jax.ShapeDtypeStruct((rows, fresh_cols), jnp.bfloat16),
        ],
        compiler_params=pltpu.CompilerParams(vmem_limit_bytes=VMEM_BYTES),
        cost_estimate=pl.CostEstimate(
            flops=4 * rows * head_cols * cache.shape[2],
            bytes_accessed=4 * cache.shape[2] * per_block * HD,
            transcendentals=rows * head_cols * 4,
        ),
        name="attend",
    )(lengths, *operands)


def output(level, batch, info, index, attended, weights, features, embeds, share_cols, held):
    dp, _, per_block, _, branch, _ = embeds.shape
    rows = dp * per_block * branch
    arrays = [w for w, _, _ in weights]
    places = [(start, side) for _, start, side in weights]
    depth = sum(w.shape[0] for w in arrays)
    keep = len(weights) > 1
    final = held is not None
    operands = [index, *attended, *arrays, features, embeds]
    in_specs = [pl.BlockSpec(memory_space=pltpu.VMEM)] * len(operands)
    scratch = [pltpu.VMEM((rows, depth), jnp.bfloat16)]
    aliases = {}
    if final:
        out_shape = [jax.ShapeDtypeStruct(held.shape, held.dtype)]
        out_specs = [pl.BlockSpec(memory_space=pl.ANY)]
        aliases = {len(operands) + 1: 0}
        operands.append(held)
        in_specs.append(pl.BlockSpec(memory_space=pl.ANY))
        scratch.append(pltpu.VMEM((dp, per_block, branch, share_cols), jnp.bfloat16))
        scratch.append(pltpu.SemaphoreType.DMA((dp,)))
    else:
        out_shape = halves(rows, share_cols)
        if keep:
            out_shape.append(pltpu.VMEM((depth, share_cols), jnp.bfloat16))
        out_specs = [pl.BlockSpec(memory_space=pltpu.VMEM)] * len(out_shape)
    return pl.pallas_call(
        functools.partial(output_kernel, level, batch, dp, places, keep, final),
        grid_spec=pltpu.PrefetchScalarGridSpec(
            num_scalar_prefetch=1,
            grid=(),
            in_specs=in_specs,
            out_specs=out_specs,
            scratch_shapes=scratch,
        ),
        out_shape=out_shape,
        input_output_aliases=aliases,
        compiler_params=pltpu.CompilerParams(vmem_limit_bytes=VMEM_BYTES),
        cost_estimate=pl.CostEstimate(
            flops=2 * rows * depth * share_cols,
            bytes_accessed=2 * rows * depth,
            transcendentals=0,
        ),
        name="output",
    )(info, *operands)


def store(level, batch, shape, info, fresh, held):
    dp, _, per_block, _, branch, share_cols = shape
    operands = [info, fresh]
    in_specs = [full(fresh)]
    aliases = {}
    if held is not None:
        in_specs.append(pl.BlockSpec(memory_space=pl.ANY))
        aliases = {2: 0}
        operands.append(held)
    return pl.pallas_call(
        store_kernel,
        grid_spec=pltpu.PrefetchScalarGridSpec(
            num_scalar_prefetch=1,
            grid=(1,),
            in_specs=in_specs,
            out_specs=pl.BlockSpec(
                (dp, 1, per_block, 1, branch, share_cols),
                lambda i, s: (0, batch, 0, level, 0, 0),
            ),
        ),
        out_shape=jax.ShapeDtypeStruct(shape, jnp.bfloat16),
        input_output_aliases=aliases,
        compiler_params=pltpu.CompilerParams(vmem_limit_bytes=VMEM_BYTES),
        cost_estimate=pl.CostEstimate(
            flops=0, bytes_accessed=4 * fresh.size, transcendentals=0
        ),
        name="store",
    )(*operands)


def shards(
    root_features,
    branch_embeds,
    parents,
    cache_lengths,
    cache_kv,
    norm_gain,
    w_query,
    w_keyval,
    w_out,
):
    requests, depths, branch, feat_cols = branch_embeds.shape
    dp, tensor, groups = (lax.axis_size(name) for name in ("dp", "tensor", "groups"))
    dp_index, tensor_index, group_index = (
        lax.axis_index(name).astype(jnp.int32) for name in ("dp", "tensor", "groups")
    )
    local = requests // dp
    batches = BATCHES
    per_block = local // batches
    share_cols = feat_cols // tensor
    head_cols = w_query.shape[1]
    head_rows = w_out.shape[0]
    by_swaps = tensor == 4 and groups == 2

    half = head_rows // 2 if by_swaps else 0
    steps = tuple(range(tensor)) if by_swaps else (0,)
    info = [dp_index ^ step for step in range(dp)]
    info += [group_index * half, (1 - group_index) * half, tensor_index]
    info += [tensor_index ^ step for step in range(tensor)] if by_swaps else [0 * dp_index]
    info = jnp.stack(info)

    if by_swaps:
        early = half * 5 // 8
        plan = ((0, 0, head_rows), (3, 0, early), (2, 0, early), (1, 0, half))
        plan += ((3, early, half - early), (2, early, half - early))
        cuts = cut(info, w_out, plan, share_cols, dp)
        info, *cuts = lax.optimization_barrier((info, *cuts))
        weights = [(cuts[0], 0, None)]
        moved = [swap(sent, "tensor", step) for sent, (step, _, _) in zip(cuts[1:4], plan[1:4])]
    else:
        spread = lax.all_to_all(w_out, "tensor", 1, 0, tiled=True)
        weights = [(load(info, spread), 0, None)]

    chosen, masks = [], []
    for batch in range(batches):
        made = prepare(batch, batches, info, parents, dp, (0,), depths, branch)
        chosen.append(made[0])
        masks.append(made[1])
    embeds = branch_embeds.reshape(dp, batches, per_block, depths, branch, feat_cols)
    gain = norm_gain.reshape(1, feat_cols)
    keyval = w_keyval.reshape(feat_cols, -1)
    w_query, keyval, embeds, cache_kv = (
        x for x in (w_query, keyval, embeds, cache_kv)
    )

    earlier = [[] for _ in range(batches)]
    shares = [root_features] * batches
    gathered = [[root_features]] * batches
    held = None
    for level in range(depths):
        attended = []
        for batch in range(batches):
            fixed = (embeds, gain, w_query, keyval)
            index = chosen[batch][level]
            pieces = gathered[batch]
            if by_swaps and level > 0:
                first = ((0, 0), (1, 0), (3, 0), (3, share_cols // 2))
                second = ((2, 0), (2, share_cols // 2))
                before = project(
                    level, batch, first, share_cols, info, index, pieces[:4], *fixed, None, False
                )[0]
                sums = project(
                    level, batch, second, share_cols, info, index, pieces[4:], *fixed, before, True
                )
            else:
                places = tuple((step, 0) for step in steps)
                cols = feat_cols // len(steps)
                sums = project(
                    level, batch, places, cols, info, index, pieces, *fixed, None, True
                )
            parts = [sums[0]] + [swap(sums[step], "dp", step) for step in range(1, dp)]
            mixed, fresh = attend(
                batch,
                per_block,
                feat_cols * dp,
                head_cols,
                cache_lengths,
                parts,
                masks[batch][level],
                cache_kv,
                earlier[batch],
            )
            earlier[batch] = earlier[batch] + [fresh]
            if level == 0:
                mixed, later = lax.optimization_barrier((mixed, info))
                made = prepare(
                    batch, batches, later, parents, dp, tuple(range(1, depths)), depths, branch
                )
                chosen[batch] += made[0]
                masks[batch] += made[1]
            if by_swaps and level == 0:
                joined = mixed
            elif by_swaps:
                heads = [mixed] + [swap(mixed, "tensor", step) for step in range(1, tensor)]
                joined = jnp.concatenate(heads, axis=1)
            else:
                joined = lax.all_gather(mixed, "tensor", axis=1, tiled=True)
            attended.append([joined] + [swap(joined, "dp", step) for step in range(1, dp)])
        for batch in range(batches):
            index = chosen[batch][level]
            if by_swaps and level == 0:
                terms = list(partial(info, attended[batch], w_out, tensor))
                sent = terms[1:]
                if batch + 1 == batches:
                    terms[0], *moved = lax.optimization_barrier((terms[0], *moved))
                    others = [swap(x, "groups", 1) for x in moved]
                terms = terms[:1] + [swap(x, "tensor", step) for step, x in enumerate(sent, 1)]
                if batch + 1 == batches:
                    terms[0], *others[:2] = lax.optimization_barrier((terms[0], *others[:2]))
                shares[batch], *split = combine(
                    level, batch, info, index, terms, shares[batch], embeds
                )
            else:
                final = level + 1 == depths
                made = output(
                    level,
                    batch,
                    info,
                    index,
                    attended[batch],
                    weights,
                    shares[batch],
                    embeds,
                    share_cols,
                    held if final else None,
                )
                if final:
                    held = made[0]
                    continue
                shares[batch], *split = made[:3]
                if len(made) > 3:
                    weights = [(made[3], 0, None)]
            held = store(
                level, batch, embeds.shape[:-1] + (share_cols,), info, shares[batch], held
            )
            own = shares[batch]
            if by_swaps:
                far, other = (swap(x, "tensor", 3) for x in split)
                if level == 0 and batch + 1 == batches:
                    other, others[2], *cuts[4:] = lax.optimization_barrier(
                        (other, others[2], *cuts[4:])
                    )
                    for sent, (step, _, _) in zip(cuts[4:], plan[4:]):
                        moved.append(swap(sent, "tensor", step))
                    others += [swap(x, "groups", 1) for x in moved[3:]]
                    for (step, start, _), one, two in zip(plan[1:], moved, others):
                        weights.append((one, step * head_rows + start, 0))
                        weights.append((two, step * head_rows + start, 1))
                near = swap(own, "tensor", 1)
                gathered[batch] = [own, near, far, other]
                gathered[batch] += [swap(far, "tensor", 1), swap(other, "tensor", 1)]
            else:
                gathered[batch] = [lax.all_gather(own, "tensor", axis=1, tiled=True)]
    return held.reshape(requests, depths, branch, share_cols)


def solution(mesh):
    return jax.shard_map(
        shards,
        mesh=mesh,
        in_specs=(
            P("groups", "dp"),
            P("groups", None, None, "dp"),
            P("groups", None, None),
            P(("groups", "dp")),
            P(("groups", "dp"), None, None, "tensor"),
            P("dp"),
            P("dp", "tensor"),
            P("dp", None, "tensor"),
            P("tensor", "dp"),
        ),
        out_specs=P("groups", None, None, ("dp", "tensor")),
        check_vma=False,
    )
```

```python
import functools

import jax
import jax.numpy as jnp
from jax import lax
from jax.experimental import pallas as pl
from jax.experimental.pallas import tpu as pltpu
from jax.sharding import PartitionSpec as P

HD = 128
BATCHES = 1
EPSILON = 1e-05
MASKED = -1e30
LANES = 128
VMEM_BYTES = 20 * 1024 * 1024


def swap(x, axis, step):
    size = lax.axis_size(axis)
    return lax.ppermute(x, axis, [(i, i ^ step) for i in range(size)])


def parent_rows(chosen_ref, features):
    return jnp.dot(chosen_ref[...], features, preferred_element_type=jnp.float32)


def embed_rows(places_ref, embed_ref, batch, level, columns):
    dp, _, per_block = embed_ref.shape[:3]
    blocks = []
    for step in range(dp):
        for request in range(per_block):
            block = embed_ref[places_ref[step], batch, request, level, :, columns]
            blocks.append(block.astype(jnp.float32))
    return jnp.concatenate(blocks, axis=0)


def cut_kernel(plan, dp, info_ref, weight_ref, *refs):
    outs, sems = refs[:-1], refs[-1]
    share = outs[0].shape[1]
    copies = []
    for place, out_ref in enumerate(outs):
        step, start, depth = plan[place]
        row = start if step == 0 else pl.multiple_of(start + info_ref[dp], 16)
        column = pl.multiple_of((info_ref[dp + 2] ^ step) * share, LANES)
        copies.append(
            pltpu.make_async_copy(
                weight_ref.at[pl.ds(row, depth), pl.ds(column, share)],
                out_ref,
                sems.at[place],
            )
        )
    for copy in copies:
        copy.start()
    for copy in copies:
        copy.wait()


def cut(info, w_out, plan, share, dp):
    shapes = [(depth, share) for _, _, depth in plan]
    return pl.pallas_call(
        functools.partial(cut_kernel, plan, dp),
        grid_spec=pltpu.PrefetchScalarGridSpec(
            num_scalar_prefetch=1,
            grid=(1,),
            in_specs=[pl.BlockSpec(memory_space=pltpu.HBM)],
            out_specs=[pl.BlockSpec(memory_space=pltpu.VMEM) for _ in shapes],
            scratch_shapes=[pltpu.SemaphoreType.DMA((len(shapes),))],
        ),
        out_shape=[pltpu.VMEM(shape, w_out.dtype) for shape in shapes],
        compiler_params=pltpu.CompilerParams(vmem_limit_bytes=VMEM_BYTES),
        name="cut",
    )(info, w_out)


def load_kernel(parts, info_ref, source_ref, held_ref, sems):
    depth = source_ref.shape[0] // parts
    copies = [
        pltpu.make_async_copy(
            source_ref.at[pl.ds(part * depth, depth)],
            held_ref.at[pl.ds(part * depth, depth)],
            sems.at[part],
        )
        for part in range(parts)
    ]
    for copy in copies:
        copy.start()
    for copy in copies:
        copy.wait()


def load(info, x):
    parts = 4
    return pl.pallas_call(
        functools.partial(load_kernel, parts),
        in_specs=[pl.BlockSpec(memory_space=pltpu.SMEM), pl.BlockSpec(memory_space=pl.ANY)],
        out_specs=pl.BlockSpec(memory_space=pltpu.VMEM),
        out_shape=pltpu.VMEM(x.shape, x.dtype),
        scratch_shapes=[pltpu.SemaphoreType.DMA((parts,))],
        compiler_params=pltpu.CompilerParams(vmem_limit_bytes=VMEM_BYTES),
        name="load",
    )(info, x)


def prepare_kernel(batch, batches, dp, levels, branch, info_ref, parents_ref, *refs):
    count = len(levels)
    chosen_refs, mask_refs, table_ref = refs[:count], refs[count : 2 * count], refs[-1]
    rows, requests = table_ref.shape[0], parents_ref.shape[0]
    local = requests // dp
    per_block = local // batches
    own = per_block * branch
    for chosen_ref, level in zip(chosen_refs, levels):
        width = chosen_ref.shape[1]
        line = lax.broadcasted_iota(jnp.int32, (branch, width), 0)
        column = lax.broadcasted_iota(jnp.int32, (branch, width), 1)
        for step in range(dp):
            for slot in range(per_block):
                request = info_ref[step] * local + batch * per_block + slot
                first = (step * per_block + slot) * branch
                if level == 0:
                    place = request
                else:
                    place = jnp.zeros((branch, width), jnp.int32)
                    for node in range(branch):
                        up = parents_ref[request, level - 1, node] + first
                        place = jnp.where(line == node, up, place)
                table_ref[first : first + branch, :width] = jnp.where(
                    column == place, 1.0, 0.0
                )
        chosen_ref[...] = table_ref[:, :width].astype(jnp.bfloat16)
    line = lax.broadcasted_iota(jnp.int32, (own, own), 0)
    column = lax.broadcasted_iota(jnp.int32, (own, own), 1)
    for mask_ref, level in zip(mask_refs, levels):
        current = jnp.where(line == column, 1.0, 0.0)
        blocks = [current]
        for upper in range(level, 0, -1):
            above = chosen_refs[upper - levels[0]][:own, :own]
            current = jnp.dot(
                current.astype(jnp.bfloat16), above, preferred_element_type=jnp.float32
            )
            blocks.insert(0, current)
        for place in range(mask_ref.shape[1] // own):
            span = slice(place * own, (place + 1) * own)
            if place < len(blocks):
                mask_ref[:, span] = blocks[place]
            else:
                mask_ref[:, span] = jnp.zeros((own, own), jnp.float32)


def prepare(batch, batches, info, parents, dp, levels, depths, branch):
    requests = parents.shape[0]
    own = requests // dp // batches * branch
    rows = dp * own
    out_shape = [
        jax.ShapeDtypeStruct((rows, rows if level else requests), jnp.bfloat16)
        for level in levels
    ]
    out_shape += [jax.ShapeDtypeStruct((own, depths * own), jnp.float32) for _ in levels]
    outs = pl.pallas_call(
        functools.partial(prepare_kernel, batch, batches, dp, levels, branch),
        in_specs=[pl.BlockSpec(memory_space=pltpu.SMEM)] * 2,
        out_specs=[pl.BlockSpec(memory_space=pltpu.VMEM)] * len(out_shape),
        out_shape=out_shape,
        scratch_shapes=[pltpu.VMEM((rows, max(rows, requests)), jnp.float32)],
        compiler_params=pltpu.CompilerParams(vmem_limit_bytes=VMEM_BYTES),
        name="prepare",
    )(info, parents)
    return list(outs[: len(levels)]), list(outs[len(levels) :])


def project_kernel(
    level, batch, places, share, spread, last, dp, info_ref, index_ref, *refs
):
    pieces = len(places) if spread else 1
    features = refs[:pieces]
    embed_ref, gain_ref, query_ref, keyval_ref = refs[pieces : pieces + 4]
    rest = refs[pieces + 4 :]
    head_cols = query_ref.shape[1]
    width = head_cols + keyval_ref.shape[1]
    query = keyval = squares = None
    for piece, place in enumerate(places):
        place, start = place
        cols = features[piece].shape[1] if spread else share
        offset = pl.multiple_of(info_ref[dp + 3 + place] * share + start, LANES)
        columns = pl.ds(offset, cols)
        held = features[piece][...] if spread else features[0][:, columns]
        state = parent_rows(index_ref, held) + embed_rows(
            info_ref, embed_ref, batch, level, columns
        )
        square = jnp.sum(state * state, axis=1, keepdims=True)
        gain = gain_ref[:, columns].astype(jnp.float32)
        scaled = (state * gain).astype(jnp.bfloat16)
        first = jnp.dot(scaled, query_ref[columns, :], preferred_element_type=jnp.float32)
        second = jnp.dot(scaled, keyval_ref[columns, :], preferred_element_type=jnp.float32)
        query = first if piece == 0 else query + first
        keyval = second if piece == 0 else keyval + second
        squares = square if piece == 0 else squares + square
    if len(rest) != (dp if last else 1):
        before_ref = rest[0]
        rest = rest[1:]
        query = query + before_ref[:, :head_cols]
        keyval = keyval + before_ref[:, head_cols:width]
        squares = squares + before_ref[:, width : width + 1]
    if not last:
        total_ref = rest[0]
        total_ref[:, :head_cols] = query
        total_ref[:, head_cols:width] = keyval
        total_ref[:, width:] = jnp.broadcast_to(squares, (squares.shape[0], LANES))
        return
    out_refs = rest
    rows = out_refs[0].shape[0]
    lane = lax.broadcasted_iota(jnp.int32, (rows, LANES), 1)
    for block in range(dp):
        span = slice(block * rows, (block + 1) * rows)
        high = squares[span].astype(jnp.bfloat16).astype(jnp.float32)
        low = squares[span] - high
        tail = jnp.where(lane == 0, high, jnp.where(lane == 1, low, 0.0))
        out_refs[block][:, :head_cols] = query[span].astype(jnp.bfloat16)
        out_refs[block][:, head_cols:width] = keyval[span].astype(jnp.bfloat16)
        out_refs[block][:, width:] = tail.astype(jnp.bfloat16)


def attend_kernel(
    dp, earlier, head_cols, model_width, base, branch, length_ref, *refs
):
    parts = refs[:dp]
    mask_ref, cache_ref = refs[dp : dp + 2]
    earlier_refs = refs[dp + 2 : dp + 2 + earlier]
    out_ref, fresh_ref = refs[dp + 2 + earlier :]
    total = parts[0][...].astype(jnp.float32)
    for part in parts[1:]:
        total = total + part[...].astype(jnp.float32)
    width = head_cols + fresh_ref.shape[1]
    squares = jnp.sum(total[:, width:], axis=1, keepdims=True)
    inv_rms = lax.rsqrt(squares / model_width + EPSILON)
    projected = (total[:, :width] * inv_rms).astype(jnp.bfloat16)
    fresh = projected[:, head_cols:]
    fresh_ref[...] = fresh
    _, _, cache, kv_cols = cache_ref.shape
    rows = total.shape[0]
    per_block = rows // branch
    kv_heads = kv_cols // HD
    group = head_cols // HD // kv_heads
    tree = [ref[...] for ref in earlier_refs] + [fresh]
    filler = mask_ref.shape[1] - rows * len(tree)
    tree += [jnp.zeros((filler, fresh.shape[1]), jnp.bfloat16)] if filler else []
    tree = jnp.concatenate(tree, axis=0)
    allowed = jnp.concatenate([mask_ref[...]] * group, axis=0) > 0.5
    column = lax.broadcasted_iota(jnp.int32, (branch, cache), 1)
    valid = [column < length_ref[base + request] for request in range(per_block)]
    across = (((1,), (1,)), ((), ()))
    scale = HD**-0.5
    for kv in range(kv_heads):
        first = kv * group
        queries = jnp.concatenate(
            [projected[:, (first + g) * HD : (first + g + 1) * HD] for g in range(group)], axis=0
        )
        key_cols = slice(kv * HD, (kv + 1) * HD)
        value_cols = slice(kv_cols + kv * HD, kv_cols + (kv + 1) * HD)
        far = lax.dot_general(
            queries, tree[:, key_cols], across, preferred_element_type=jnp.float32
        )
        far = jnp.where(allowed, far * scale, MASKED)
        found = []
        for request in range(per_block):
            keys = cache_ref[base + request, 0, :, key_cols]
            scores = lax.dot_general(queries, keys, across, preferred_element_type=jnp.float32)
            found.append(scores)
        blocks = []
        for g in range(group):
            for request in range(per_block):
                start = g * rows + request * branch
                block = found[request][start : start + branch] * scale
                blocks.append(jnp.where(valid[request], block, MASKED))
        near = jnp.concatenate(blocks, axis=0)
        top = jnp.maximum(
            jnp.max(near, axis=1, keepdims=True), jnp.max(far, axis=1, keepdims=True)
        )
        near = jnp.exp(near - top)
        far = jnp.exp(far - top)
        below = jnp.sum(near, axis=1, keepdims=True) + jnp.sum(far, axis=1, keepdims=True)
        near = (near / below).astype(jnp.bfloat16)
        far = (far / below).astype(jnp.bfloat16)
        mixed = jnp.dot(far, tree[:, value_cols], preferred_element_type=jnp.float32)
        found = []
        for request in range(per_block):
            values = cache_ref[base + request, 1, :, key_cols]
            found.append(jnp.dot(near, values, preferred_element_type=jnp.float32))
        for g in range(group):
            blocks = []
            for request in range(per_block):
                start = g * rows + request * branch
                blocks.append(
                    found[request][start : start + branch] + mixed[start : start + branch]
                )
            block = jnp.concatenate(blocks, axis=0).astype(jnp.bfloat16)
            out_ref[:, (first + g) * HD : (first + g + 1) * HD] = block


def output_kernel(level, batch, dp, weights, keep, final, info_ref, index_ref, *refs):
    attended = refs[:dp]
    weight_refs = refs[dp : dp + len(weights)]
    feature_ref, embed_ref = refs[dp + len(weights) : dp + len(weights) + 2]
    rest = refs[dp + len(weights) + 2 :]
    rows = attended[0].shape[0]
    if final:
        _, held_ref, gathered_ref, staged_ref, sems = rest
        share = staged_ref.shape[3]
    else:
        kept, gathered_ref = rest[-2], rest[-1]
        out_refs = rest[:-2] if keep else rest[:-1]
        share = out_refs[0].shape[1]
    for step in range(dp):
        gathered_ref[step * rows : (step + 1) * rows, :] = attended[step][...]
    spans = []
    for weight_ref, (start, side) in zip(weight_refs, weights):
        depth = weight_ref.shape[0]
        if side is not None:
            start = pl.multiple_of(start + info_ref[dp + side], LANES // 4)
        spans.append(pl.ds(start, depth))
        if keep:
            kept[spans[-1], :] = weight_ref[...]
    if keep:
        weight_refs = [kept]
    offset = pl.multiple_of(info_ref[dp + 2] * share, LANES)
    block = min(2 * LANES, share)
    for start in range(0, share, block):
        if feature_ref.shape[1] == share:
            held = feature_ref[:, start : start + block]
        else:
            held = feature_ref[:, pl.ds(offset + start, block)]
        fresh = parent_rows(index_ref, held) + embed_rows(
            info_ref, embed_ref, batch, level, pl.ds(offset + start, block)
        )
        fresh = fresh + jnp.dot(
            gathered_ref[...],
            weight_refs[0][:, start : start + block],
            preferred_element_type=jnp.float32,
        )
        if not final:
            write_halves(fresh.astype(jnp.bfloat16), start, out_refs)
            continue
        branch = staged_ref.shape[2]
        for step in range(dp):
            for request in range(staged_ref.shape[1]):
                first = (step * staged_ref.shape[1] + request) * branch
                staged_ref[step, request, :, start : start + block] = fresh[
                    first : first + branch
                ].astype(jnp.bfloat16)
    if final:
        copies = [
            pltpu.make_async_copy(
                staged_ref.at[step],
                held_ref.at[info_ref[step], batch, :, level],
                sems.at[step],
            )
            for step in range(dp)
        ]
        for copy in copies:
            copy.start()
        for copy in copies:
            copy.wait()


def store_kernel(info_ref, fresh_ref, *refs):
    out_ref = refs[-1]
    dp, per_block, branch = out_ref.shape[0], out_ref.shape[2], out_ref.shape[4]
    fresh = fresh_ref[...].astype(jnp.float32)
    for step in range(dp):
        for request in range(per_block):
            start = (step * per_block + request) * branch
            block = fresh[start : start + branch].astype(jnp.bfloat16)
            out_ref[info_ref[step], 0, request, 0] = block


def partial_kernel(dp, info_ref, *refs):
    attended, weight_ref = refs[:dp], refs[dp]
    outs = refs[dp + 1 :]
    left = jnp.concatenate([ref[...] for ref in attended], axis=0)
    share = outs[0].shape[1]
    block = min(4 * LANES, share)
    for place, out_ref in enumerate(outs):
        offset = pl.multiple_of(info_ref[dp + 3 + place] * share, LANES)
        for start in range(0, share, block):
            out_ref[:, start : start + block] = jnp.dot(
                left,
                weight_ref[:, pl.ds(offset + start, block)],
                preferred_element_type=jnp.float32,
            ).astype(jnp.bfloat16)


def partial(info, attended, w_out, shares):
    dp = len(attended)
    rows = dp * attended[0].shape[0]
    share_cols = w_out.shape[1] // shares
    operands = [*attended, w_out]
    return pl.pallas_call(
        functools.partial(partial_kernel, dp),
        grid_spec=pltpu.PrefetchScalarGridSpec(
            num_scalar_prefetch=1,
            grid=(),
            in_specs=[pl.BlockSpec(memory_space=pltpu.VMEM)] * len(operands),
            out_specs=[pl.BlockSpec(memory_space=pltpu.VMEM)] * shares,
        ),
        out_shape=[jax.ShapeDtypeStruct((rows, share_cols), jnp.bfloat16)] * shares,
        compiler_params=pltpu.CompilerParams(vmem_limit_bytes=VMEM_BYTES),
        name="partial",
    )(info, *operands)


def add_kernel(first_ref, second_ref, out_ref):
    total = first_ref[...].astype(jnp.float32) + second_ref[...].astype(jnp.float32)
    out_ref[...] = total.astype(jnp.bfloat16)


def add(first, second):
    return pl.pallas_call(
        add_kernel,
        in_specs=[pl.BlockSpec(memory_space=pltpu.VMEM)] * 2,
        out_specs=pl.BlockSpec(memory_space=pltpu.VMEM),
        out_shape=jax.ShapeDtypeStruct(first.shape, first.dtype),
        compiler_params=pltpu.CompilerParams(vmem_limit_bytes=VMEM_BYTES),
        name="add",
    )(first, second)


def combine_kernel(level, batch, dp, info_ref, index_ref, *refs):
    terms, (feature_ref, embed_ref, *out_refs) = refs[:-5], refs[-5:]
    share = out_refs[0].shape[1]
    offset = pl.multiple_of(info_ref[dp + 2] * share, LANES)
    columns = pl.ds(offset, share)
    fresh = parent_rows(index_ref, feature_ref[:, columns]) + embed_rows(
        info_ref, embed_ref, batch, level, columns
    )
    for term in terms:
        fresh = fresh + term[...].astype(jnp.float32)
    write_halves(fresh.astype(jnp.bfloat16), 0, out_refs)


def write_halves(fresh, start, out_refs):
    width = fresh.shape[1]
    out_refs[0][:, start : start + width] = fresh
    for half_ref in out_refs[1:]:
        half = half_ref.shape[1]
        low, high = max(start, 0), min(start + width, half)
        if low < high:
            half_ref[:, low:high] = fresh[:, low - start : high - start]
        start -= half


def halves(rows, share_cols):
    shapes = [(rows, share_cols), (rows, share_cols // 2), (rows, share_cols // 2)]
    return [jax.ShapeDtypeStruct(shape, jnp.bfloat16) for shape in shapes]


def combine(level, batch, info, index, terms, features, embeds):
    operands = [index, *terms, features, embeds]
    return pl.pallas_call(
        functools.partial(combine_kernel, level, batch, embeds.shape[0]),
        grid_spec=pltpu.PrefetchScalarGridSpec(
            num_scalar_prefetch=1,
            grid=(),
            in_specs=[pl.BlockSpec(memory_space=pltpu.VMEM)] * len(operands),
            out_specs=[pl.BlockSpec(memory_space=pltpu.VMEM)] * 3,
        ),
        out_shape=halves(*terms[0].shape),
        compiler_params=pltpu.CompilerParams(vmem_limit_bytes=VMEM_BYTES),
        name="combine",
    )(info, *operands)


def store_kernel(info_ref, fresh_ref, *refs):
    out_ref = refs[-1]
    dp, per_block, branch = out_ref.shape[0], out_ref.shape[2], out_ref.shape[4]
    fresh = fresh_ref[...].astype(jnp.float32)
    for step in range(dp):
        for request in range(per_block):
            start = (step * per_block + request) * branch
            block = fresh[start : start + branch].astype(jnp.bfloat16)
            out_ref[info_ref[step], 0, request, 0] = block


def full(x):
    return pl.BlockSpec(x.shape, lambda i, *_: (0,) * x.ndim)


def project(
    level, batch, places, share, info, index, pieces, embeds, gain, w_query, keyval, before, last
):
    dp, _, per_block, _, branch, feat_cols = embeds.shape
    head_cols, kv_cols = w_query.shape[1], keyval.shape[1]
    rows = per_block * branch
    width = head_cols + kv_cols + LANES
    operands = [index, *pieces, embeds, gain, w_query, keyval]
    operands += [] if before is None else [before]
    if last:
        out_shape = [jax.ShapeDtypeStruct((rows, width), jnp.bfloat16)] * dp
    else:
        out_shape = [jax.ShapeDtypeStruct((dp * rows, width), jnp.float32)]
    spread = level > 0 and len(pieces) == len(places)
    return pl.pallas_call(
        functools.partial(project_kernel, level, batch, places, share, spread, last, dp),
        grid_spec=pltpu.PrefetchScalarGridSpec(
            num_scalar_prefetch=1,
            grid=(),
            in_specs=[pl.BlockSpec(memory_space=pltpu.VMEM)] * len(operands),
            out_specs=[pl.BlockSpec(memory_space=pltpu.VMEM)] * len(out_shape),
        ),
        out_shape=out_shape,
        compiler_params=pltpu.CompilerParams(vmem_limit_bytes=VMEM_BYTES),
        cost_estimate=pl.CostEstimate(
            flops=2 * dp * rows * feat_cols * (head_cols + kv_cols),
            bytes_accessed=4 * dp * rows * feat_cols,
            transcendentals=0,
        ),
        name="project",
    )(info, *operands)


def attend(batch, per_block, model_width, head_cols, lengths, parts, mask, cache, earlier):
    rows, width = parts[0].shape
    fresh_cols = width - LANES - head_cols
    operands = [*parts, mask, cache, *earlier]
    return pl.pallas_call(
        functools.partial(
            attend_kernel,
            len(parts),
            len(earlier),
            head_cols,
            model_width,
            batch * per_block,
            rows // per_block,
        ),
        grid_spec=pltpu.PrefetchScalarGridSpec(
            num_scalar_prefetch=1,
            grid=(),
            in_specs=[pl.BlockSpec(memory_space=pltpu.VMEM)] * len(operands),
            out_specs=[pl.BlockSpec(memory_space=pltpu.VMEM)] * 2,
        ),
        out_shape=[
            jax.ShapeDtypeStruct((rows, head_cols), jnp.bfloat16),
            jax.ShapeDtypeStruct((rows, fresh_cols), jnp.bfloat16),
        ],
        compiler_params=pltpu.CompilerParams(vmem_limit_bytes=VMEM_BYTES),
        cost_estimate=pl.CostEstimate(
            flops=4 * rows * head_cols * cache.shape[2],
            bytes_accessed=4 * cache.shape[2] * per_block * HD,
            transcendentals=rows * head_cols * 4,
        ),
        name="attend",
    )(lengths, *operands)


def output(level, batch, info, index, attended, weights, features, embeds, share_cols, held):
    dp, _, per_block, _, branch, _ = embeds.shape
    rows = dp * per_block * branch
    arrays = [w for w, _, _ in weights]
    places = [(start, side) for _, start, side in weights]
    depth = sum(w.shape[0] for w in arrays)
    keep = len(weights) > 1
    final = held is not None
    operands = [index, *attended, *arrays, features, embeds]
    in_specs = [pl.BlockSpec(memory_space=pltpu.VMEM)] * len(operands)
    scratch = [pltpu.VMEM((rows, depth), jnp.bfloat16)]
    aliases = {}
    if final:
        out_shape = [jax.ShapeDtypeStruct(held.shape, held.dtype)]
        out_specs = [pl.BlockSpec(memory_space=pl.ANY)]
        aliases = {len(operands) + 1: 0}
        operands.append(held)
        in_specs.append(pl.BlockSpec(memory_space=pl.ANY))
        scratch.append(pltpu.VMEM((dp, per_block, branch, share_cols), jnp.bfloat16))
        scratch.append(pltpu.SemaphoreType.DMA((dp,)))
    else:
        out_shape = halves(rows, share_cols)
        if keep:
            out_shape.append(pltpu.VMEM((depth, share_cols), jnp.bfloat16))
        out_specs = [pl.BlockSpec(memory_space=pltpu.VMEM)] * len(out_shape)
    return pl.pallas_call(
        functools.partial(output_kernel, level, batch, dp, places, keep, final),
        grid_spec=pltpu.PrefetchScalarGridSpec(
            num_scalar_prefetch=1,
            grid=(),
            in_specs=in_specs,
            out_specs=out_specs,
            scratch_shapes=scratch,
        ),
        out_shape=out_shape,
        input_output_aliases=aliases,
        compiler_params=pltpu.CompilerParams(vmem_limit_bytes=VMEM_BYTES),
        cost_estimate=pl.CostEstimate(
            flops=2 * rows * depth * share_cols,
            bytes_accessed=2 * rows * depth,
            transcendentals=0,
        ),
        name="output",
    )(info, *operands)


def store(level, batch, shape, info, fresh, held):
    dp, _, per_block, _, branch, share_cols = shape
    operands = [info, fresh]
    in_specs = [full(fresh)]
    aliases = {}
    if held is not None:
        in_specs.append(pl.BlockSpec(memory_space=pl.ANY))
        aliases = {2: 0}
        operands.append(held)
    return pl.pallas_call(
        store_kernel,
        grid_spec=pltpu.PrefetchScalarGridSpec(
            num_scalar_prefetch=1,
            grid=(1,),
            in_specs=in_specs,
            out_specs=pl.BlockSpec(
                (dp, 1, per_block, 1, branch, share_cols),
                lambda i, s: (0, batch, 0, level, 0, 0),
            ),
        ),
        out_shape=jax.ShapeDtypeStruct(shape, jnp.bfloat16),
        input_output_aliases=aliases,
        compiler_params=pltpu.CompilerParams(vmem_limit_bytes=VMEM_BYTES),
        cost_estimate=pl.CostEstimate(
            flops=0, bytes_accessed=4 * fresh.size, transcendentals=0
        ),
        name="store",
    )(*operands)


def shards(
    root_features,
    branch_embeds,
    parents,
    cache_lengths,
    cache_kv,
    norm_gain,
    w_query,
    w_keyval,
    w_out,
):
    requests, depths, branch, feat_cols = branch_embeds.shape
    dp, tensor, groups = (lax.axis_size(name) for name in ("dp", "tensor", "groups"))
    dp_index, tensor_index, group_index = (
        lax.axis_index(name).astype(jnp.int32) for name in ("dp", "tensor", "groups")
    )
    local = requests // dp
    batches = BATCHES
    per_block = local // batches
    share_cols = feat_cols // tensor
    head_cols = w_query.shape[1]
    head_rows = w_out.shape[0]
    by_swaps = tensor == 4 and groups == 2

    half = head_rows // 2 if by_swaps else 0
    steps = tuple(range(tensor)) if by_swaps else (0,)
    info = [dp_index ^ step for step in range(dp)]
    info += [group_index * half, (1 - group_index) * half, tensor_index]
    info += [tensor_index ^ step for step in range(tensor)] if by_swaps else [0 * dp_index]
    info = jnp.stack(info)

    if by_swaps:
        chunk = half * 3 // 8
        plan = ((3, 0, half), (1, 0, half), (2, 0, chunk), (2, chunk, half - chunk))
        plan += ((0, 0, head_rows),)
        source = pltpu.with_memory_space_constraint(w_out, pltpu.HBM)
        cuts = cut(info, source, plan[:3], share_cols, dp)
        info, *cuts = lax.optimization_barrier((info, *cuts))
        moved = [swap(sent, "tensor", step) for sent, (step, _, _) in zip(cuts, plan)]
    else:
        spread = lax.all_to_all(w_out, "tensor", 1, 0, tiled=True)
        weights = [(load(info, spread), 0, None)]

    chosen, masks = [], []
    for batch in range(batches):
        made = prepare(batch, batches, info, parents, dp, (0,), depths, branch)
        chosen.append(made[0])
        masks.append(made[1])
    embeds = branch_embeds.reshape(dp, batches, per_block, depths, branch, feat_cols)
    gain = norm_gain.reshape(1, feat_cols)
    keyval = w_keyval.reshape(feat_cols, -1)
    w_query, keyval, embeds, cache_kv = (
        x for x in (w_query, keyval, embeds, cache_kv)
    )

    earlier = [[] for _ in range(batches)]
    shares = [root_features] * batches
    gathered = [[root_features]] * batches
    held = None
    for level in range(depths):
        attended = []
        for batch in range(batches):
            fixed = (embeds, gain, w_query, keyval)
            index = chosen[batch][level]
            pieces = gathered[batch]
            if by_swaps and level > 0:
                first = ((0, 0), (1, 0), (3, 0), (3, share_cols // 2))
                second = ((2, 0), (2, share_cols // 2))
                before = project(
                    level, batch, first, share_cols, info, index, pieces[:4], *fixed, None, False
                )[0]
                sums = project(
                    level, batch, second, share_cols, info, index, pieces[4:], *fixed, before, True
                )
            else:
                places = tuple((step, 0) for step in steps)
                cols = feat_cols // len(steps)
                sums = project(
                    level, batch, places, cols, info, index, pieces, *fixed, None, True
                )
            sums = list(sums)
            if by_swaps and level == 0 and batch + 1 == batches:
                sums[0], later = lax.optimization_barrier((sums[0], info))
                cuts = list(cut(later, source, plan[3:], share_cols, dp))
                weights = [(cuts[1], 0, None)]
                sums[0], cuts[0] = lax.optimization_barrier((sums[0], cuts[0]))
            parts = [sums[0]] + [swap(sums[step], "dp", step) for step in range(1, dp)]
            mixed, fresh = attend(
                batch,
                per_block,
                feat_cols * dp,
                head_cols,
                cache_lengths,
                parts,
                masks[batch][level],
                cache_kv,
                earlier[batch],
            )
            earlier[batch] = earlier[batch] + [fresh]
            if level == 0:
                mixed, later = lax.optimization_barrier((mixed, info))
                made = prepare(
                    batch, batches, later, parents, dp, tuple(range(1, depths)), depths, branch
                )
                chosen[batch] += made[0]
                masks[batch] += made[1]
            if by_swaps and level == 0:
                joined = mixed
            elif by_swaps:
                heads = [mixed] + [swap(mixed, "tensor", step) for step in range(1, tensor)]
                joined = jnp.concatenate(heads, axis=1)
            else:
                joined = lax.all_gather(mixed, "tensor", axis=1, tiled=True)
            attended.append([joined] + [swap(joined, "dp", step) for step in range(1, dp)])
        for batch in range(batches):
            index = chosen[batch][level]
            if by_swaps and level == 0:
                terms = list(partial(info, attended[batch], w_out, tensor))
                own, near, other, far = terms
                other = swap(other, "tensor", 1)
                if batch + 1 == batches:
                    own, *moved[:2] = lax.optimization_barrier((own, *moved[:2]))
                    others = [swap(x, "groups", 1) for x in moved[:2]]
                if batch + 1 == batches:
                    far, moved[2] = lax.optimization_barrier((far, moved[2]))
                far = swap(add(far, other), "tensor", 3)
                near = swap(near, "tensor", 1)
                own, *chosen[batch][1:] = lax.optimization_barrier((own, *chosen[batch][1:]))
                terms = [own, near, far]
                shares[batch], *split = combine(
                    level, batch, info, index, terms, shares[batch], embeds
                )
            else:
                final = level + 1 == depths
                made = output(
                    level,
                    batch,
                    info,
                    index,
                    attended[batch],
                    weights,
                    shares[batch],
                    embeds,
                    share_cols,
                    held if final else None,
                )
                if final:
                    held = made[0]
                    continue
                shares[batch], *split = made[:3]
                if len(made) > 3:
                    weights = [(made[3], 0, None)]
            held = store(
                level, batch, embeds.shape[:-1] + (share_cols,), info, shares[batch], held
            )
            own = shares[batch]
            if by_swaps:
                far, other = (swap(x, "tensor", 3) for x in split)
                first = level == 0 and batch + 1 == batches
                if first:
                    far, other, moved[2], *others = lax.optimization_barrier(
                        (far, other, moved[2], *others)
                    )
                    others.append(swap(moved[2], "groups", 1))
                near = swap(own, "tensor", 1)
                last = [swap(far, "tensor", 1), swap(other, "tensor", 1)]
                if first:
                    *last, cuts[0] = lax.optimization_barrier((*last, cuts[0]))
                    moved.append(swap(cuts[0], "tensor", 2))
                    others.append(swap(moved[3], "groups", 1))
                    for (step, start, _), one, two in zip(plan, moved, others):
                        weights.append((one, step * head_rows + start, 0))
                        weights.append((two, step * head_rows + start, 1))
                gathered[batch] = [own, near, far, other, *last]
            else:
                gathered[batch] = [lax.all_gather(own, "tensor", axis=1, tiled=True)]
    return held.reshape(requests, depths, branch, share_cols)


def solution(mesh):
    return jax.shard_map(
        shards,
        mesh=mesh,
        in_specs=(
            P("groups", "dp"),
            P("groups", None, None, "dp"),
            P("groups", None, None),
            P(("groups", "dp")),
            P(("groups", "dp"), None, None, "tensor"),
            P("dp"),
            P("dp", "tensor"),
            P("dp", None, "tensor"),
            P("tensor", "dp"),
        ),
        out_specs=P("groups", None, None, ("dp", "tensor")),
        check_vma=False,
    )
```

```python
import functools

import jax
import jax.numpy as jnp
from jax import lax
from jax.experimental import pallas as pl
from jax.experimental.pallas import tpu as pltpu
from jax.sharding import PartitionSpec as P

HD = 128
BATCHES = 1
EPSILON = 1e-05
MASKED = -1e30
LANES = 128
VMEM_BYTES = 20 * 1024 * 1024


def swap(x, axis, step):
    size = lax.axis_size(axis)
    return lax.ppermute(x, axis, [(i, i ^ step) for i in range(size)])


def parent_rows(chosen_ref, features):
    return jnp.dot(chosen_ref[...], features, preferred_element_type=jnp.float32)


def embed_rows(places_ref, embed_ref, batch, level, columns):
    dp, _, per_block = embed_ref.shape[:3]
    blocks = []
    for step in range(dp):
        for request in range(per_block):
            block = embed_ref[places_ref[step], batch, request, level, :, columns]
            blocks.append(block.astype(jnp.float32))
    return jnp.concatenate(blocks, axis=0)


def cut_kernel(plan, dp, info_ref, weight_ref, *refs):
    outs, sems = refs[:-1], refs[-1]
    share = outs[0].shape[1]
    copies = []
    for place, out_ref in enumerate(outs):
        step, start, depth = plan[place]
        row = start if step == 0 else pl.multiple_of(start + info_ref[dp], 16)
        column = pl.multiple_of((info_ref[dp + 2] ^ step) * share, LANES)
        copies.append(
            pltpu.make_async_copy(
                weight_ref.at[pl.ds(row, depth), pl.ds(column, share)],
                out_ref,
                sems.at[place],
            )
        )
    for copy in copies:
        copy.start()
    for copy in copies:
        copy.wait()


def cut(info, w_out, plan, share, dp):
    shapes = [(depth, share) for _, _, depth in plan]
    return pl.pallas_call(
        functools.partial(cut_kernel, plan, dp),
        grid_spec=pltpu.PrefetchScalarGridSpec(
            num_scalar_prefetch=1,
            grid=(1,),
            in_specs=[pl.BlockSpec(memory_space=pltpu.HBM)],
            out_specs=[pl.BlockSpec(memory_space=pltpu.VMEM) for _ in shapes],
            scratch_shapes=[pltpu.SemaphoreType.DMA((len(shapes),))],
        ),
        out_shape=[pltpu.VMEM(shape, w_out.dtype) for shape in shapes],
        compiler_params=pltpu.CompilerParams(vmem_limit_bytes=VMEM_BYTES),
        name="cut",
    )(info, w_out)


def load_kernel(parts, info_ref, source_ref, held_ref, sems):
    depth = source_ref.shape[0] // parts
    copies = [
        pltpu.make_async_copy(
            source_ref.at[pl.ds(part * depth, depth)],
            held_ref.at[pl.ds(part * depth, depth)],
            sems.at[part],
        )
        for part in range(parts)
    ]
    for copy in copies:
        copy.start()
    for copy in copies:
        copy.wait()


def load(info, x):
    parts = 4
    return pl.pallas_call(
        functools.partial(load_kernel, parts),
        in_specs=[pl.BlockSpec(memory_space=pltpu.SMEM), pl.BlockSpec(memory_space=pl.ANY)],
        out_specs=pl.BlockSpec(memory_space=pltpu.VMEM),
        out_shape=pltpu.VMEM(x.shape, x.dtype),
        scratch_shapes=[pltpu.SemaphoreType.DMA((parts,))],
        compiler_params=pltpu.CompilerParams(vmem_limit_bytes=VMEM_BYTES),
        name="load",
    )(info, x)


def prepare_kernel(batch, batches, dp, levels, branch, info_ref, parents_ref, *refs):
    count = len(levels)
    chosen_refs, mask_refs, table_ref = refs[:count], refs[count : 2 * count], refs[-1]
    rows, requests = table_ref.shape[0], parents_ref.shape[0]
    local = requests // dp
    per_block = local // batches
    own = per_block * branch
    for chosen_ref, level in zip(chosen_refs, levels):
        width = chosen_ref.shape[1]
        line = lax.broadcasted_iota(jnp.int32, (branch, width), 0)
        column = lax.broadcasted_iota(jnp.int32, (branch, width), 1)
        for step in range(dp):
            for slot in range(per_block):
                request = info_ref[step] * local + batch * per_block + slot
                first = (step * per_block + slot) * branch
                if level == 0:
                    place = request
                else:
                    place = jnp.zeros((branch, width), jnp.int32)
                    for node in range(branch):
                        up = parents_ref[request, level - 1, node] + first
                        place = jnp.where(line == node, up, place)
                table_ref[first : first + branch, :width] = jnp.where(
                    column == place, 1.0, 0.0
                )
        chosen_ref[...] = table_ref[:, :width].astype(jnp.bfloat16)
    line = lax.broadcasted_iota(jnp.int32, (own, own), 0)
    column = lax.broadcasted_iota(jnp.int32, (own, own), 1)
    for mask_ref, level in zip(mask_refs, levels):
        current = jnp.where(line == column, 1.0, 0.0)
        blocks = [current]
        for upper in range(level, 0, -1):
            above = chosen_refs[upper - levels[0]][:own, :own]
            current = jnp.dot(
                current.astype(jnp.bfloat16), above, preferred_element_type=jnp.float32
            )
            blocks.insert(0, current)
        for place in range(mask_ref.shape[1] // own):
            span = slice(place * own, (place + 1) * own)
            if place < len(blocks):
                mask_ref[:, span] = blocks[place]
            else:
                mask_ref[:, span] = jnp.zeros((own, own), jnp.float32)


def prepare(batch, batches, info, parents, dp, levels, depths, branch):
    requests = parents.shape[0]
    own = requests // dp // batches * branch
    rows = dp * own
    out_shape = [
        jax.ShapeDtypeStruct((rows, rows if level else requests), jnp.bfloat16)
        for level in levels
    ]
    out_shape += [jax.ShapeDtypeStruct((own, depths * own), jnp.float32) for _ in levels]
    outs = pl.pallas_call(
        functools.partial(prepare_kernel, batch, batches, dp, levels, branch),
        in_specs=[pl.BlockSpec(memory_space=pltpu.SMEM)] * 2,
        out_specs=[pl.BlockSpec(memory_space=pltpu.VMEM)] * len(out_shape),
        out_shape=out_shape,
        scratch_shapes=[pltpu.VMEM((rows, max(rows, requests)), jnp.float32)],
        compiler_params=pltpu.CompilerParams(vmem_limit_bytes=VMEM_BYTES),
        name="prepare",
    )(info, parents)
    return list(outs[: len(levels)]), list(outs[len(levels) :])


def project_kernel(
    level, batch, places, share, spread, last, dp, info_ref, index_ref, *refs
):
    pieces = len(places) if spread else 1
    features = refs[:pieces]
    embed_ref, gain_ref, query_ref, keyval_ref = refs[pieces : pieces + 4]
    rest = refs[pieces + 4 :]
    head_cols = query_ref.shape[1]
    width = head_cols + keyval_ref.shape[1]
    query = keyval = squares = None
    for piece, place in enumerate(places):
        place, start = place
        cols = features[piece].shape[1] if spread else share
        offset = pl.multiple_of(info_ref[dp + 3 + place] * share + start, LANES)
        columns = pl.ds(offset, cols)
        held = features[piece][...] if spread else features[0][:, columns]
        state = parent_rows(index_ref, held) + embed_rows(
            info_ref, embed_ref, batch, level, columns
        )
        square = jnp.sum(state * state, axis=1, keepdims=True)
        gain = gain_ref[:, columns].astype(jnp.float32)
        scaled = (state * gain).astype(jnp.bfloat16)
        first = jnp.dot(scaled, query_ref[columns, :], preferred_element_type=jnp.float32)
        second = jnp.dot(scaled, keyval_ref[columns, :], preferred_element_type=jnp.float32)
        query = first if piece == 0 else query + first
        keyval = second if piece == 0 else keyval + second
        squares = square if piece == 0 else squares + square
    if len(rest) != (dp if last else 1):
        before_ref = rest[0]
        rest = rest[1:]
        query = query + before_ref[:, :head_cols]
        keyval = keyval + before_ref[:, head_cols:width]
        squares = squares + before_ref[:, width : width + 1]
    if not last:
        total_ref = rest[0]
        total_ref[:, :head_cols] = query
        total_ref[:, head_cols:width] = keyval
        total_ref[:, width:] = jnp.broadcast_to(squares, (squares.shape[0], LANES))
        return
    out_refs = rest
    rows = out_refs[0].shape[0]
    lane = lax.broadcasted_iota(jnp.int32, (rows, LANES), 1)
    for block in range(dp):
        span = slice(block * rows, (block + 1) * rows)
        high = squares[span].astype(jnp.bfloat16).astype(jnp.float32)
        low = squares[span] - high
        tail = jnp.where(lane == 0, high, jnp.where(lane == 1, low, 0.0))
        out_refs[block][:, :head_cols] = query[span].astype(jnp.bfloat16)
        out_refs[block][:, head_cols:width] = keyval[span].astype(jnp.bfloat16)
        out_refs[block][:, width:] = tail.astype(jnp.bfloat16)


def attend_kernel(
    dp, earlier, head_cols, model_width, base, branch, length_ref, *refs
):
    parts = refs[:dp]
    mask_ref, cache_ref = refs[dp : dp + 2]
    earlier_refs = refs[dp + 2 : dp + 2 + earlier]
    out_ref, fresh_ref = refs[dp + 2 + earlier :]
    total = parts[0][...].astype(jnp.float32)
    for part in parts[1:]:
        total = total + part[...].astype(jnp.float32)
    width = head_cols + fresh_ref.shape[1]
    squares = jnp.sum(total[:, width:], axis=1, keepdims=True)
    inv_rms = lax.rsqrt(squares / model_width + EPSILON)
    projected = (total[:, :width] * inv_rms).astype(jnp.bfloat16)
    fresh = projected[:, head_cols:]
    fresh_ref[...] = fresh
    _, _, cache, kv_cols = cache_ref.shape
    rows = total.shape[0]
    per_block = rows // branch
    kv_heads = kv_cols // HD
    group = head_cols // HD // kv_heads
    tree = [ref[...] for ref in earlier_refs] + [fresh]
    filler = mask_ref.shape[1] - rows * len(tree)
    tree += [jnp.zeros((filler, fresh.shape[1]), jnp.bfloat16)] if filler else []
    tree = jnp.concatenate(tree, axis=0)
    allowed = jnp.concatenate([mask_ref[...]] * group, axis=0) > 0.5
    column = lax.broadcasted_iota(jnp.int32, (branch, cache), 1)
    valid = [column < length_ref[base + request] for request in range(per_block)]
    across = (((1,), (1,)), ((), ()))
    scale = HD**-0.5
    for kv in range(kv_heads):
        first = kv * group
        queries = jnp.concatenate(
            [projected[:, (first + g) * HD : (first + g + 1) * HD] for g in range(group)], axis=0
        )
        key_cols = slice(kv * HD, (kv + 1) * HD)
        value_cols = slice(kv_cols + kv * HD, kv_cols + (kv + 1) * HD)
        far = lax.dot_general(
            queries, tree[:, key_cols], across, preferred_element_type=jnp.float32
        )
        far = jnp.where(allowed, far * scale, MASKED)
        found = []
        for request in range(per_block):
            keys = cache_ref[base + request, 0, :, key_cols]
            scores = lax.dot_general(queries, keys, across, preferred_element_type=jnp.float32)
            found.append(scores)
        blocks = []
        for g in range(group):
            for request in range(per_block):
                start = g * rows + request * branch
                block = found[request][start : start + branch] * scale
                blocks.append(jnp.where(valid[request], block, MASKED))
        near = jnp.concatenate(blocks, axis=0)
        top = jnp.maximum(
            jnp.max(near, axis=1, keepdims=True), jnp.max(far, axis=1, keepdims=True)
        )
        near = jnp.exp(near - top)
        far = jnp.exp(far - top)
        below = jnp.sum(near, axis=1, keepdims=True) + jnp.sum(far, axis=1, keepdims=True)
        near = (near / below).astype(jnp.bfloat16)
        far = (far / below).astype(jnp.bfloat16)
        mixed = jnp.dot(far, tree[:, value_cols], preferred_element_type=jnp.float32)
        found = []
        for request in range(per_block):
            values = cache_ref[base + request, 1, :, key_cols]
            found.append(jnp.dot(near, values, preferred_element_type=jnp.float32))
        for g in range(group):
            blocks = []
            for request in range(per_block):
                start = g * rows + request * branch
                blocks.append(
                    found[request][start : start + branch] + mixed[start : start + branch]
                )
            block = jnp.concatenate(blocks, axis=0).astype(jnp.bfloat16)
            out_ref[:, (first + g) * HD : (first + g + 1) * HD] = block


def output_kernel(level, batch, dp, weights, keep, final, info_ref, index_ref, *refs):
    attended = refs[:dp]
    weight_refs = refs[dp : dp + len(weights)]
    feature_ref, embed_ref = refs[dp + len(weights) : dp + len(weights) + 2]
    rest = refs[dp + len(weights) + 2 :]
    rows = attended[0].shape[0]
    if final:
        _, held_ref, gathered_ref, staged_ref, sems = rest
        share = staged_ref.shape[3]
    else:
        kept, gathered_ref = rest[-2], rest[-1]
        out_refs = rest[:-2] if keep else rest[:-1]
        share = out_refs[0].shape[1]
    for step in range(dp):
        gathered_ref[step * rows : (step + 1) * rows, :] = attended[step][...]
    spans = []
    for weight_ref, (start, side) in zip(weight_refs, weights):
        depth = weight_ref.shape[0]
        if side is not None:
            start = pl.multiple_of(start + info_ref[dp + side], LANES // 4)
        spans.append(pl.ds(start, depth))
        if keep:
            kept[spans[-1], :] = weight_ref[...]
    if keep:
        weight_refs = [kept]
    offset = pl.multiple_of(info_ref[dp + 2] * share, LANES)
    block = min(2 * LANES, share)
    for start in range(0, share, block):
        if feature_ref.shape[1] == share:
            held = feature_ref[:, start : start + block]
        else:
            held = feature_ref[:, pl.ds(offset + start, block)]
        fresh = parent_rows(index_ref, held) + embed_rows(
            info_ref, embed_ref, batch, level, pl.ds(offset + start, block)
        )
        fresh = fresh + jnp.dot(
            gathered_ref[...],
            weight_refs[0][:, start : start + block],
            preferred_element_type=jnp.float32,
        )
        if not final:
            write_halves(fresh.astype(jnp.bfloat16), start, out_refs)
            continue
        branch = staged_ref.shape[2]
        for step in range(dp):
            for request in range(staged_ref.shape[1]):
                first = (step * staged_ref.shape[1] + request) * branch
                staged_ref[step, request, :, start : start + block] = fresh[
                    first : first + branch
                ].astype(jnp.bfloat16)
    if final:
        copies = [
            pltpu.make_async_copy(
                staged_ref.at[step],
                held_ref.at[info_ref[step], batch, :, level],
                sems.at[step],
            )
            for step in range(dp)
        ]
        for copy in copies:
            copy.start()
        for copy in copies:
            copy.wait()


def store_kernel(info_ref, fresh_ref, *refs):
    out_ref = refs[-1]
    dp, per_block, branch = out_ref.shape[0], out_ref.shape[2], out_ref.shape[4]
    fresh = fresh_ref[...].astype(jnp.float32)
    for step in range(dp):
        for request in range(per_block):
            start = (step * per_block + request) * branch
            block = fresh[start : start + branch].astype(jnp.bfloat16)
            out_ref[info_ref[step], 0, request, 0] = block


def partial_kernel(dp, info_ref, *refs):
    attended, weight_ref = refs[:dp], refs[dp]
    outs = refs[dp + 1 :]
    left = jnp.concatenate([ref[...] for ref in attended], axis=0)
    share = outs[0].shape[1]
    block = min(4 * LANES, share)
    for place, out_ref in enumerate(outs):
        offset = pl.multiple_of(info_ref[dp + 3 + place] * share, LANES)
        for start in range(0, share, block):
            out_ref[:, start : start + block] = jnp.dot(
                left,
                weight_ref[:, pl.ds(offset + start, block)],
                preferred_element_type=jnp.float32,
            ).astype(jnp.bfloat16)


def partial(info, attended, w_out, shares):
    dp = len(attended)
    rows = dp * attended[0].shape[0]
    share_cols = w_out.shape[1] // shares
    operands = [*attended, w_out]
    return pl.pallas_call(
        functools.partial(partial_kernel, dp),
        grid_spec=pltpu.PrefetchScalarGridSpec(
            num_scalar_prefetch=1,
            grid=(),
            in_specs=[pl.BlockSpec(memory_space=pltpu.VMEM)] * len(operands),
            out_specs=[pl.BlockSpec(memory_space=pltpu.VMEM)] * shares,
        ),
        out_shape=[jax.ShapeDtypeStruct((rows, share_cols), jnp.bfloat16)] * shares,
        compiler_params=pltpu.CompilerParams(vmem_limit_bytes=VMEM_BYTES),
        name="partial",
    )(info, *operands)


def add_kernel(first_ref, second_ref, out_ref):
    total = first_ref[...].astype(jnp.float32) + second_ref[...].astype(jnp.float32)
    out_ref[...] = total.astype(jnp.bfloat16)


def add(first, second):
    return pl.pallas_call(
        add_kernel,
        in_specs=[pl.BlockSpec(memory_space=pltpu.VMEM)] * 2,
        out_specs=pl.BlockSpec(memory_space=pltpu.VMEM),
        out_shape=jax.ShapeDtypeStruct(first.shape, first.dtype),
        compiler_params=pltpu.CompilerParams(vmem_limit_bytes=VMEM_BYTES),
        name="add",
    )(first, second)


def combine_kernel(level, batch, dp, info_ref, index_ref, *refs):
    terms, (feature_ref, embed_ref, *out_refs) = refs[:-5], refs[-5:]
    share = out_refs[0].shape[1]
    offset = pl.multiple_of(info_ref[dp + 2] * share, LANES)
    columns = pl.ds(offset, share)
    fresh = parent_rows(index_ref, feature_ref[:, columns]) + embed_rows(
        info_ref, embed_ref, batch, level, columns
    )
    for term in terms:
        fresh = fresh + term[...].astype(jnp.float32)
    write_halves(fresh.astype(jnp.bfloat16), 0, out_refs)


def write_halves(fresh, start, out_refs):
    width = fresh.shape[1]
    out_refs[0][:, start : start + width] = fresh
    for half_ref in out_refs[1:]:
        half = half_ref.shape[1]
        low, high = max(start, 0), min(start + width, half)
        if low < high:
            half_ref[:, low:high] = fresh[:, low - start : high - start]
        start -= half


def halves(rows, share_cols):
    shapes = [(rows, share_cols), (rows, share_cols // 2), (rows, share_cols // 2)]
    return [jax.ShapeDtypeStruct(shape, jnp.bfloat16) for shape in shapes]


def combine(level, batch, info, index, terms, features, embeds):
    operands = [index, *terms, features, embeds]
    return pl.pallas_call(
        functools.partial(combine_kernel, level, batch, embeds.shape[0]),
        grid_spec=pltpu.PrefetchScalarGridSpec(
            num_scalar_prefetch=1,
            grid=(),
            in_specs=[pl.BlockSpec(memory_space=pltpu.VMEM)] * len(operands),
            out_specs=[pl.BlockSpec(memory_space=pltpu.VMEM)] * 3,
        ),
        out_shape=halves(*terms[0].shape),
        compiler_params=pltpu.CompilerParams(vmem_limit_bytes=VMEM_BYTES),
        name="combine",
    )(info, *operands)


def store_kernel(info_ref, fresh_ref, *refs):
    out_ref = refs[-1]
    dp, per_block, branch = out_ref.shape[0], out_ref.shape[2], out_ref.shape[4]
    fresh = fresh_ref[...].astype(jnp.float32)
    for step in range(dp):
        for request in range(per_block):
            start = (step * per_block + request) * branch
            block = fresh[start : start + branch].astype(jnp.bfloat16)
            out_ref[info_ref[step], 0, request, 0] = block


def full(x):
    return pl.BlockSpec(x.shape, lambda i, *_: (0,) * x.ndim)


def project(
    level, batch, places, share, info, index, pieces, embeds, gain, w_query, keyval, before, last
):
    dp, _, per_block, _, branch, feat_cols = embeds.shape
    head_cols, kv_cols = w_query.shape[1], keyval.shape[1]
    rows = per_block * branch
    width = head_cols + kv_cols + LANES
    operands = [index, *pieces, embeds, gain, w_query, keyval]
    operands += [] if before is None else [before]
    if last:
        out_shape = [jax.ShapeDtypeStruct((rows, width), jnp.bfloat16)] * dp
    else:
        out_shape = [jax.ShapeDtypeStruct((dp * rows, width), jnp.float32)]
    spread = level > 0 and len(pieces) == len(places)
    return pl.pallas_call(
        functools.partial(project_kernel, level, batch, places, share, spread, last, dp),
        grid_spec=pltpu.PrefetchScalarGridSpec(
            num_scalar_prefetch=1,
            grid=(),
            in_specs=[pl.BlockSpec(memory_space=pltpu.VMEM)] * len(operands),
            out_specs=[pl.BlockSpec(memory_space=pltpu.VMEM)] * len(out_shape),
        ),
        out_shape=out_shape,
        compiler_params=pltpu.CompilerParams(vmem_limit_bytes=VMEM_BYTES),
        cost_estimate=pl.CostEstimate(
            flops=2 * dp * rows * feat_cols * (head_cols + kv_cols),
            bytes_accessed=4 * dp * rows * feat_cols,
            transcendentals=0,
        ),
        name="project",
    )(info, *operands)


def attend(batch, per_block, model_width, head_cols, lengths, parts, mask, cache, earlier):
    rows, width = parts[0].shape
    fresh_cols = width - LANES - head_cols
    operands = [*parts, mask, cache, *earlier]
    return pl.pallas_call(
        functools.partial(
            attend_kernel,
            len(parts),
            len(earlier),
            head_cols,
            model_width,
            batch * per_block,
            rows // per_block,
        ),
        grid_spec=pltpu.PrefetchScalarGridSpec(
            num_scalar_prefetch=1,
            grid=(),
            in_specs=[pl.BlockSpec(memory_space=pltpu.VMEM)] * len(operands),
            out_specs=[pl.BlockSpec(memory_space=pltpu.VMEM)] * 2,
        ),
        out_shape=[
            jax.ShapeDtypeStruct((rows, head_cols), jnp.bfloat16),
            jax.ShapeDtypeStruct((rows, fresh_cols), jnp.bfloat16),
        ],
        compiler_params=pltpu.CompilerParams(vmem_limit_bytes=VMEM_BYTES),
        cost_estimate=pl.CostEstimate(
            flops=4 * rows * head_cols * cache.shape[2],
            bytes_accessed=4 * cache.shape[2] * per_block * HD,
            transcendentals=rows * head_cols * 4,
        ),
        name="attend",
    )(lengths, *operands)


def output(level, batch, info, index, attended, weights, features, embeds, share_cols, held):
    dp, _, per_block, _, branch, _ = embeds.shape
    rows = dp * per_block * branch
    arrays = [w for w, _, _ in weights]
    places = [(start, side) for _, start, side in weights]
    depth = sum(w.shape[0] for w in arrays)
    keep = len(weights) > 1
    final = held is not None
    operands = [index, *attended, *arrays, features, embeds]
    in_specs = [pl.BlockSpec(memory_space=pltpu.VMEM)] * len(operands)
    scratch = [pltpu.VMEM((rows, depth), jnp.bfloat16)]
    aliases = {}
    if final:
        out_shape = [jax.ShapeDtypeStruct(held.shape, held.dtype)]
        out_specs = [pl.BlockSpec(memory_space=pl.ANY)]
        aliases = {len(operands) + 1: 0}
        operands.append(held)
        in_specs.append(pl.BlockSpec(memory_space=pl.ANY))
        scratch.append(pltpu.VMEM((dp, per_block, branch, share_cols), jnp.bfloat16))
        scratch.append(pltpu.SemaphoreType.DMA((dp,)))
    else:
        out_shape = halves(rows, share_cols)
        if keep:
            out_shape.append(pltpu.VMEM((depth, share_cols), jnp.bfloat16))
        out_specs = [pl.BlockSpec(memory_space=pltpu.VMEM)] * len(out_shape)
    return pl.pallas_call(
        functools.partial(output_kernel, level, batch, dp, places, keep, final),
        grid_spec=pltpu.PrefetchScalarGridSpec(
            num_scalar_prefetch=1,
            grid=(),
            in_specs=in_specs,
            out_specs=out_specs,
            scratch_shapes=scratch,
        ),
        out_shape=out_shape,
        input_output_aliases=aliases,
        compiler_params=pltpu.CompilerParams(vmem_limit_bytes=VMEM_BYTES),
        cost_estimate=pl.CostEstimate(
            flops=2 * rows * depth * share_cols,
            bytes_accessed=2 * rows * depth,
            transcendentals=0,
        ),
        name="output",
    )(info, *operands)


def store(level, batch, shape, info, fresh, held):
    dp, _, per_block, _, branch, share_cols = shape
    operands = [info, fresh]
    in_specs = [full(fresh)]
    aliases = {}
    if held is not None:
        in_specs.append(pl.BlockSpec(memory_space=pl.ANY))
        aliases = {2: 0}
        operands.append(held)
    return pl.pallas_call(
        store_kernel,
        grid_spec=pltpu.PrefetchScalarGridSpec(
            num_scalar_prefetch=1,
            grid=(1,),
            in_specs=in_specs,
            out_specs=pl.BlockSpec(
                (dp, 1, per_block, 1, branch, share_cols),
                lambda i, s: (0, batch, 0, level, 0, 0),
            ),
        ),
        out_shape=jax.ShapeDtypeStruct(shape, jnp.bfloat16),
        input_output_aliases=aliases,
        compiler_params=pltpu.CompilerParams(vmem_limit_bytes=VMEM_BYTES),
        cost_estimate=pl.CostEstimate(
            flops=0, bytes_accessed=4 * fresh.size, transcendentals=0
        ),
        name="store",
    )(*operands)


def shards(
    root_features,
    branch_embeds,
    parents,
    cache_lengths,
    cache_kv,
    norm_gain,
    w_query,
    w_keyval,
    w_out,
):
    requests, depths, branch, feat_cols = branch_embeds.shape
    dp, tensor, groups = (lax.axis_size(name) for name in ("dp", "tensor", "groups"))
    dp_index, tensor_index, group_index = (
        lax.axis_index(name).astype(jnp.int32) for name in ("dp", "tensor", "groups")
    )
    local = requests // dp
    batches = BATCHES
    per_block = local // batches
    share_cols = feat_cols // tensor
    head_cols = w_query.shape[1]
    head_rows = w_out.shape[0]
    by_swaps = tensor == 4 and groups == 2

    half = head_rows // 2 if by_swaps else 0
    steps = tuple(range(tensor)) if by_swaps else (0,)
    info = [dp_index ^ step for step in range(dp)]
    info += [group_index * half, (1 - group_index) * half, tensor_index]
    info += [tensor_index ^ step for step in range(tensor)] if by_swaps else [0 * dp_index]
    info = jnp.stack(info)

    if by_swaps:
        chunk = half * 3 // 8
        plan = ((3, 0, half), (1, 0, half), (2, 0, chunk), (2, chunk, half - chunk))
        plan += ((0, 0, head_rows),)
        source = pltpu.with_memory_space_constraint(w_out, pltpu.HBM)
        cuts = cut(info, source, plan[:3], share_cols, dp)
        info, *cuts = lax.optimization_barrier((info, *cuts))
        moved = [swap(sent, "tensor", step) for sent, (step, _, _) in zip(cuts, plan)]
    else:
        spread = lax.all_to_all(w_out, "tensor", 1, 0, tiled=True)
        weights = [(load(info, spread), 0, None)]

    chosen, masks = [], []
    for batch in range(batches):
        made = prepare(batch, batches, info, parents, dp, (0,), depths, branch)
        chosen.append(made[0])
        masks.append(made[1])
    embeds = branch_embeds.reshape(dp, batches, per_block, depths, branch, feat_cols)
    gain = norm_gain.reshape(1, feat_cols)
    keyval = w_keyval.reshape(feat_cols, -1)
    w_query, keyval, embeds, cache_kv = (
        x for x in (w_query, keyval, embeds, cache_kv)
    )

    earlier = [[] for _ in range(batches)]
    shares = [root_features] * batches
    gathered = [[root_features]] * batches
    held = None
    for level in range(depths):
        attended = []
        for batch in range(batches):
            fixed = (embeds, gain, w_query, keyval)
            index = chosen[batch][level]
            pieces = gathered[batch]
            if by_swaps and level > 0:
                first = ((0, 0), (1, 0), (3, 0), (3, share_cols // 2))
                second = ((2, 0), (2, share_cols // 2))
                before = project(
                    level, batch, first, share_cols, info, index, pieces[:4], *fixed, None, False
                )[0]
                before, held = lax.optimization_barrier((before, held))
                sums = project(
                    level, batch, second, share_cols, info, index, pieces[4:], *fixed, before, True
                )
            else:
                places = tuple((step, 0) for step in steps)
                cols = feat_cols // len(steps)
                sums = project(
                    level, batch, places, cols, info, index, pieces, *fixed, None, True
                )
            sums = list(sums)
            if by_swaps and level == 0 and batch + 1 == batches:
                sums[0], later = lax.optimization_barrier((sums[0], info))
                cuts = list(cut(later, source, plan[3:], share_cols, dp))
                weights = [(cuts[1], 0, None)]
                sums[0], cuts[0] = lax.optimization_barrier((sums[0], cuts[0]))
            parts = [sums[0]] + [swap(sums[step], "dp", step) for step in range(1, dp)]
            mixed, fresh = attend(
                batch,
                per_block,
                feat_cols * dp,
                head_cols,
                cache_lengths,
                parts,
                masks[batch][level],
                cache_kv,
                earlier[batch],
            )
            earlier[batch] = earlier[batch] + [fresh]
            if level == 0:
                mixed, later = lax.optimization_barrier((mixed, info))
                made = prepare(
                    batch, batches, later, parents, dp, tuple(range(1, depths)), depths, branch
                )
                chosen[batch] += made[0]
                masks[batch] += made[1]
            if by_swaps and level == 0:
                joined = mixed
            elif by_swaps:
                heads = [mixed] + [swap(mixed, "tensor", step) for step in range(1, tensor)]
                joined = jnp.concatenate(heads, axis=1)
            else:
                joined = lax.all_gather(mixed, "tensor", axis=1, tiled=True)
            if dp == 4 and level > 1:
                across = swap(joined, "dp", 2)
                attended.append([joined, swap(joined, "dp", 1), across, swap(across, "dp", 1)])
            else:
                attended.append([joined] + [swap(joined, "dp", step) for step in range(1, dp)])
        for batch in range(batches):
            index = chosen[batch][level]
            if by_swaps and level == 0:
                terms = list(partial(info, attended[batch], w_out, tensor))
                own, near, other, far = terms
                other = swap(other, "tensor", 1)
                if batch + 1 == batches:
                    own, *moved[:2] = lax.optimization_barrier((own, *moved[:2]))
                    others = [swap(x, "groups", 1) for x in moved[:2]]
                if batch + 1 == batches:
                    far, moved[2] = lax.optimization_barrier((far, moved[2]))
                far = swap(add(far, other), "tensor", 3)
                near = swap(near, "tensor", 1)
                own, *chosen[batch][1:] = lax.optimization_barrier((own, *chosen[batch][1:]))
                terms = [own, near, far]
                shares[batch], *split = combine(
                    level, batch, info, index, terms, shares[batch], embeds
                )
            else:
                final = level + 1 == depths
                made = output(
                    level,
                    batch,
                    info,
                    index,
                    attended[batch],
                    weights,
                    shares[batch],
                    embeds,
                    share_cols,
                    held if final else None,
                )
                if final:
                    held = made[0]
                    continue
                shares[batch], *split = made[:3]
                if len(made) > 3:
                    weights = [(made[3], 0, None)]
            held = store(
                level, batch, embeds.shape[:-1] + (share_cols,), info, shares[batch], held
            )
            own = shares[batch]
            if by_swaps:
                far, other = (swap(x, "tensor", 3) for x in split)
                first = level == 0 and batch + 1 == batches
                if first:
                    far, other, moved[2], *others = lax.optimization_barrier(
                        (far, other, moved[2], *others)
                    )
                    others.append(swap(moved[2], "groups", 1))
                near = swap(own, "tensor", 1)
                last = [swap(far, "tensor", 1), swap(other, "tensor", 1)]
                if first:
                    *last, cuts[0] = lax.optimization_barrier((*last, cuts[0]))
                    moved.append(swap(cuts[0], "tensor", 2))
                    others.append(swap(moved[3], "groups", 1))
                    for (step, start, _), one, two in zip(plan, moved, others):
                        weights.append((one, step * head_rows + start, 0))
                        weights.append((two, step * head_rows + start, 1))
                gathered[batch] = [own, near, far, other, *last]
            else:
                gathered[batch] = [lax.all_gather(own, "tensor", axis=1, tiled=True)]
    return held.reshape(requests, depths, branch, share_cols)


def solution(mesh):
    return jax.shard_map(
        shards,
        mesh=mesh,
        in_specs=(
            P("groups", "dp"),
            P("groups", None, None, "dp"),
            P("groups", None, None),
            P(("groups", "dp")),
            P(("groups", "dp"), None, None, "tensor"),
            P("dp"),
            P("dp", "tensor"),
            P("dp", None, "tensor"),
            P("tensor", "dp"),
        ),
        out_specs=P("groups", None, None, ("dp", "tensor")),
        check_vma=False,
    )
```
